32 devices in a mesh: edata: 16 (over z, y, x), llm: 2 (over core).
Axes of the slice: x: 2, y: 2, z: 4, core: 2. Of those that a mesh axis runs over, the one named last changes fastest.
Arguments:
- grad_rows: bfloat16 [2048, 3200], P(('edata', 'llm')), may hold values from -6 to 6
- row_target: int32 [2048, 1], P(('edata', 'llm')), may hold values from 0 to 15; in each aligned block of 64 rows (0 to 63, 64 to 127, ...) at most 5 rows name the same one
- stored_context: bfloat16 [2560, 2048], P('edata', 'llm'), may hold values from -448 to 448
- block_scale: float32 [2560, 16], P('edata', 'llm'), may hold values from 0.002 to 0.008
- w_out: bfloat16 [2048, 3200], P('llm', 'edata'), may hold values from -0.125 to 0.125
- layer_scale: float32 [3200], replicated, may hold values from 0.3 to 3
Outputs:
- grad_context: bfloat16 [2560, 2048], P('edata', 'llm')
- grad_weight: float32 [3200, 2048], P('edata', 'llm')
- grad_scale: float32 [3200], replicated
The draws below stay inside these ranges and needn't reach their ends.
Inputs may be any that keep to these rules, and one draw needn't show every extreme that they name: `row_target`: among the 64 rows of one device, no encoder device is named by more than 5 rows, and some encoder device is named by exactly 5 rows.
All inputs are finite; a program needn't handle non-finite values.
Results may differ from the reference program's by a relative error of at most 0.0049.
Values may be sent and summed in bfloat16 or wider, within the bound.
A program may use at most 128 MiB of HBM per device.

```python
import math
import jax
import jax.numpy as jnp
import numpy as np
from jax import lax

WIDTH = 3200
BLOCK = 128
SRC_DEV = 64
CTX = 2048
CAP = 5
SLOTS = 160
ROWS = 2048
N_EDATA = 16
N_LLM = 2


def steps_of(own_key, extent, pieces, smallest, top_value):
    gain, own = 1.0, jax.random.fold_in(own_key, 6)
    for position, blocks in pieces:
        heights = jnp.exp(jax.random.uniform(jax.random.fold_in(own, position), (blocks,), jnp.float32, smallest / len(pieces), top_value / len(pieces)))
        gain = gain * jnp.repeat(heights, extent[position] // blocks).reshape([-1 if axis == position else 1 for axis in range(len(extent))])
    return gain


def shared_out(key, own, number, rows, number_of, top, reach, slope):
    ranking = jax.random.permutation(key, number_of)
    heavy_load, usual = portions_of(number_of, rows * top, reach, slope, True), portions_of(number_of, rows * top, reach, slope, False)
    places = jnp.arange(number_of)

    def named(sizes, offset_by):
        used = int((sizes > 0).sum())
        fixed = max(1, used // 4)
        passed = fixed + (places - fixed + offset_by * (used - fixed)) % max(1, number_of - fixed)
        return jnp.zeros((number_of,), jnp.int32).at[ranking[jnp.where(places < fixed, places, passed)]].set(jnp.asarray(sizes, jnp.int32))

    sizes = jnp.where(number % 4 == 0, named(heavy_load, number // 4), named(usual, number - number // 4 - 1))
    mixed = jax.random.permutation(jax.random.fold_in(own, 3), number_of)
    source_of, receiver = mixed[0:number_of // 2 * 2:2], mixed[1:number_of // 2 * 2:2]
    slack = jnp.minimum(sizes[source_of] - 1, reach - sizes[receiver]) // 2
    slack = jnp.where((source_of == ranking[0]) | (receiver == ranking[0]) | (sizes[receiver] == 0), 0, jnp.maximum(slack, 0))
    passed = jax.random.randint(jax.random.fold_in(own, 4), (number_of // 2,), 0, 1 << 20) % (slack + 1)
    sizes = sizes.at[source_of].add(-passed).at[receiver].add(passed)
    labels = jnp.searchsorted(jnp.cumsum(sizes), jnp.arange(rows * top), side="right").astype(jnp.int32)
    grid = labels.reshape(top, rows).T
    grid = grid[jax.random.permutation(jax.random.fold_in(own, 1), rows)]
    offset_by = jax.random.randint(jax.random.fold_in(own, 2), (rows, 1), 0, top)
    return jnp.take_along_axis(grid, (jnp.arange(top)[None, :] + offset_by) % top, axis=1)


def portions_of(number_of, total, reach, lean, full):
    portions = [(1 << 20) // math.isqrt(rank ** lean) + 1 for rank in range(1, number_of + 1)]
    largest = reach if full else min(reach, max(-(-total // number_of), total * portions[0] // sum(portions)))
    least = 1 if total - largest >= number_of - 1 else 0
    given, surplus = [largest] + [least] * (number_of - 1), total - largest - least * (number_of - 1)
    while surplus > 0:
        candidates = [i for i in range(1, number_of) if given[i] < largest] or [i for i in range(1, number_of) if given[i] < reach]
        mass, budget = sum([portions[i] for i in candidates]), surplus
        for i in candidates:
            addition = min(reach - given[i], max(1, budget * portions[i] // mass), surplus)
            given[i] = given[i] + addition
            surplus = surplus - addition
    return np.array(given)


def noise(stream_key, dims, deviation, reach, shards=(), kind=jnp.bfloat16):
    loudness = steps_of(stream_key, dims, shards, -0.22, 0.18) if shards else 1.0
    array = jax.random.normal(stream_key, dims, jnp.float32) * deviation * loudness
    return jnp.minimum(jnp.maximum(array, -reach), reach).astype(kind)


def setup_inputs(seed: int = 0) -> dict:
    streams_of = jax.random.split(jax.random.key(seed), 7)
    grad_rows = noise(streams_of[0], (ROWS, WIDTH), 1.0, 6.0, ((0, 32),))
    row_target_keys = jax.random.split(jax.random.fold_in(streams_of[1], 1), ROWS // SRC_DEV)
    row_target_turns = jax.random.permutation(jax.random.fold_in(streams_of[1], 3), ROWS // SRC_DEV)
    row_target = jax.vmap(lambda own, number: shared_out(jax.random.fold_in(streams_of[1], 2), own, number, SRC_DEV, N_EDATA, 1, CAP, 2))(row_target_keys, row_target_turns).reshape((ROWS, 1))
    stored_context = jnp.clip(jax.random.uniform(streams_of[2], (N_EDATA * SLOTS, CTX), jnp.float32, -448.0, 448.0) * steps_of(streams_of[2], (N_EDATA * SLOTS, CTX), ((0, 16), (1, 2)), -0.4, 0.0), -448.0, 448.0).astype(jnp.bfloat16)
    block_scale = jnp.clip(jnp.exp(math.log(0.008) - 1.3862944 * jax.random.uniform(streams_of[3], (N_EDATA * SLOTS, CTX // BLOCK), jnp.float32) ** steps_of(streams_of[3], (N_EDATA * SLOTS, CTX // BLOCK), ((0, 16), (1, 2)), -0.2, 0.2)), 0.002, 0.008)
    w_out = noise(streams_of[4], (CTX, WIDTH), CTX ** -0.5, 0.125, ((0, 2), (1, 16)))
    layer_scale = jnp.clip(jnp.exp(jax.random.uniform(streams_of[5], (WIDTH,), jnp.float32, math.log(0.3), math.log(3.0))), 0.3, 3.0)
    return {"grad_rows": grad_rows, "row_target": row_target, "stored_context": stored_context, "block_scale": block_scale, "w_out": w_out, "layer_scale": layer_scale}


def reference(grad_rows, row_target, stored_context, block_scale, w_out, layer_scale):
    targets = row_target[:, 0].reshape(N_EDATA, N_LLM, SRC_DEV)
    chosen = (targets[..., None] == jnp.arange(N_EDATA, dtype=jnp.int32)).astype(jnp.int32)
    arrival = lax.optimization_barrier(jnp.sum(chosen * (jnp.cumsum(chosen, axis=2) - 1), axis=3)).astype(jnp.int32)
    source_enc = jnp.arange(N_EDATA, dtype=jnp.int32)[:, None, None]
    source_own = jnp.arange(N_LLM, dtype=jnp.int32)[None, :, None]
    slot_index = (source_own * N_EDATA + source_enc) * CAP + arrival
    placed = (targets * SLOTS + slot_index).reshape(ROWS).astype(jnp.int32)
    stored = stored_context[placed].astype(jnp.float32).reshape(ROWS, CTX // BLOCK, BLOCK)
    context = (stored * block_scale[placed][:, :, None]).reshape(ROWS, CTX).astype(jnp.bfloat16)
    scaled = (grad_rows.astype(jnp.float32) * layer_scale[None, :]).astype(jnp.bfloat16)
    recomputed = jnp.dot(context, w_out, preferred_element_type=jnp.float32)
    live_grad = jnp.dot(scaled, w_out.T, preferred_element_type=jnp.float32).astype(jnp.bfloat16)
    grad_context = jnp.zeros((N_EDATA * SLOTS, CTX), jnp.bfloat16).at[placed].set(live_grad)
    rescale = 1.0 / math.sqrt(ROWS)
    grad_weight = jnp.dot(scaled.T, context, preferred_element_type=jnp.float32) * rescale
    grad_scale = lax.optimization_barrier(jnp.sum(grad_rows.astype(jnp.float32) * recomputed, axis=0)) * rescale
    return (grad_context, grad_weight, grad_scale)
```

```python
import functools
import math

import jax
import jax.numpy as jnp
from jax import lax
from jax.experimental import pallas as pl
from jax.experimental.pallas import tpu as pltpu
from jax.sharding import PartitionSpec as P

BLOCK = 128
GROUP = 4
MESH = pl.DeviceIdType.MESH


def up(value, unit):
    return -(-value // unit) * unit


def kernel(
    capacity, rescale, rows_ref, place_ref, context_ref, weight_ref,
    grad_context_ref, grad_weight_ref, scale_ref,
    row_buf, place_buf, routed, arrived, grads, grads_t, contexts, weights,
    context_out, context_in, weight_out, weight_in, scale_pair, scale_group,
    row_send, row_recv, place_send, place_recv, context_send, context_recv,
    weight_send, weight_recv, routed_send, routed_recv, gc_send, gc_recv,
    gw_send, gw_recv, pair_send, pair_recv, group_send, group_recv, all_send, all_recv,
):
    e, core = lax.axis_index("edata"), lax.axis_index("llm")
    depth, plane = e // GROUP, e % GROUP
    other = 1 - core
    features = weight_ref.shape[0]
    slots = context_ref.shape[0]
    block = routed.shape[1]

    def ahead(own, k):
        return (own + k) % GROUP

    def along_depth(k):
        return (ahead(depth, k) * GROUP + plane, core)

    def along_plane(k, owner):
        return (depth * GROUP + ahead(plane, k), owner)

    def send(src, dst, send_sem, recv_sem, device):
        return pltpu.make_async_remote_copy(
            src_ref=src, dst_ref=dst, send_sem=send_sem, recv_sem=recv_sem,
            device_id=device, device_id_type=MESH,
        )

    barrier = pltpu.get_barrier_semaphore()
    for k in range(1, GROUP):
        pl.semaphore_signal(barrier, inc=1, device_id=along_depth(k), device_id_type=MESH)
        for owner in (core, other):
            pl.semaphore_signal(
                barrier, inc=1, device_id=along_plane(k, owner), device_id_type=MESH
            )
    pl.semaphore_signal(barrier, inc=1, device_id=(e, other), device_id_type=MESH)
    pl.semaphore_wait(barrier, 3 * (GROUP - 1) + 1)

    row_copies = []
    place_copies = []
    for k in range(1, GROUP):
        row_copies.append(
            send(rows_ref.at[ahead(depth, k)], row_buf.at[depth],
                 row_send.at[k - 1], row_recv.at[k - 1], along_depth(k))
        )
        place_copies.append(
            send(place_ref, place_buf.at[depth],
                 place_send.at[k - 1], place_recv.at[k - 1], along_depth(k))
        )
    for copy in place_copies + row_copies:
        copy.start()
    weight_copies = [
        send(weight_ref, weights.at[plane], weight_send.at[k - 1], weight_recv.at[k - 1],
             along_plane(k, core))
        for k in range(1, GROUP)
    ]
    for copy in weight_copies:
        copy.start()
    context_copies = [
        send(context_ref, contexts.at[depth], context_send.at[k - 1], context_recv.at[k - 1],
             along_depth(k))
        for k in range(1, GROUP)
    ]
    for copy in context_copies:
        copy.start()
    row_buf[depth] = rows_ref[depth]
    place_buf[depth] = place_ref[...]
    weights[plane] = weight_ref[...]
    contexts[depth] = context_ref[...]

    for copy in place_copies:
        copy.wait()
    places = place_buf[0, 0:1, :]
    for j in range(1, GROUP):
        places = places + place_buf[j, 0:1, :]
    source_rows = row_buf.shape[1]
    width = row_buf.shape[2]
    wanted = lax.broadcasted_iota(jnp.int32, (GROUP * block, GROUP * source_rows), 0)
    choice = jnp.where(wanted == places, 1.0, 0.0).astype(jnp.bfloat16)
    for copy in row_copies:
        copy.wait()
    routed[...] = (
        jnp.dot(
            choice, row_buf[...].reshape(GROUP * source_rows, width),
            preferred_element_type=jnp.float32,
        )
        .astype(jnp.bfloat16)
        .reshape(GROUP, block, width)
    )
    mine = core * GROUP + plane
    routed_copies = []
    for k in range(1, GROUP):
        for which, owner in enumerate((core, other)):
            index = 2 * (k - 1) + which
            routed_copies.append(
                send(routed.at[ahead(plane, k)], arrived.at[mine],
                     routed_send.at[index], routed_recv.at[index], along_plane(k, owner))
            )
    routed_copies.append(
        send(routed.at[plane], arrived.at[mine], routed_send.at[2 * (GROUP - 1)],
             routed_recv.at[2 * (GROUP - 1)], (e, other))
    )
    for copy in routed_copies:
        copy.start()
    arrived[mine] = routed[plane]

    total = GROUP * slots
    slot = lax.broadcasted_iota(jnp.int32, (total, 1), 0)
    fifth = (slot * (2**18 // capacity + 1)) >> 18
    arrival = slot - fifth * capacity
    plane_of, source_depth = fifth & 3, (fifth >> 2) & 3
    core_of, target_depth = (fifth >> 4) & 1, fifth >> 5
    found = (
        (core_of * GROUP + plane_of) * block
        + (target_depth * GROUP + source_depth) * capacity
        + arrival
    )
    order = jnp.where(
        lax.broadcasted_iota(jnp.int32, (total, total), 1) == found, 1.0, 0.0
    ).astype(jnp.bfloat16)
    for copy in routed_copies:
        copy.wait()
    ordered = jnp.dot(
        order, arrived[...].reshape(total, width), preferred_element_type=jnp.float32
    )
    grads[...] = ordered.astype(jnp.bfloat16).reshape(GROUP, slots, width)
    grads_t[...] = (
        ordered.T[: GROUP * features, :].astype(jnp.bfloat16).reshape(GROUP, features, total)
    )

    for copy in weight_copies:
        copy.wait()

    def gc_copy(k):
        return send(context_out.at[ahead(depth, k)], context_in.at[depth],
                    gc_send.at[k - 1], gc_recv.at[k - 1], along_depth(k))

    def context_step(k, carry):
        at = ahead(depth, k)
        context_out[at] = jnp.dot(
            grads[at][:, : GROUP * features],
            weights[...].reshape(GROUP * features, -1),
            preferred_element_type=jnp.float32,
        ).astype(jnp.bfloat16)

        @pl.when(k < GROUP)
        def _():
            gc_copy(k).start()

        return carry

    lax.fori_loop(1, GROUP + 1, context_step, 0)

    for copy in context_copies:
        copy.wait()

    def gw_copy(k):
        return send(weight_out.at[ahead(plane, k)], weight_in.at[plane],
                    gw_send.at[k - 1], gw_recv.at[k - 1], along_plane(k, core))

    def weight_step(k, carry):
        at = ahead(plane, k)
        weight_out[at] = jnp.dot(
            grads_t[at], contexts[...].reshape(total, -1), preferred_element_type=jnp.float32
        ).astype(jnp.bfloat16)

        @pl.when(k < GROUP)
        def _():
            gw_copy(k).start()

        return carry

    lax.fori_loop(1, GROUP + 1, weight_step, 0)

    for k in range(1, GROUP):
        gw_copy(k).wait()
    summed = weight_out[plane].astype(jnp.float32)
    for k in range(1, GROUP):
        summed = summed + weight_in[ahead(plane, GROUP - k)].astype(jnp.float32)
    real = grad_weight_ref.shape[0]
    grad_weight_ref[...] = summed[:real, :] * rescale
    product = summed * weight_ref[...].astype(jnp.float32)
    lanes = product[:, :BLOCK]
    for j in range(1, product.shape[1] // BLOCK):
        lanes = lanes + product[:, j * BLOCK : (j + 1) * BLOCK]
    own = jnp.sum(lanes.T, axis=0, keepdims=True) * rescale
    pad = scale_pair.shape[2] - features
    own = jnp.broadcast_to(jnp.pad(own, ((0, 0), (0, pad))), scale_pair.shape[1:])

    scale_pair[0] = own
    pair = send(scale_pair.at[0], scale_pair.at[1], pair_send.at[0], pair_recv.at[0], (e, other))
    pair.start()
    pair.wait()
    scale_group[plane] = scale_pair[0] + scale_pair[1]
    group_copies = [
        send(scale_group.at[plane], scale_group.at[plane], group_send.at[k - 1],
             group_recv.at[k - 1], along_plane(k, core))
        for k in range(1, GROUP)
    ]
    for copy in group_copies:
        copy.start()
    for copy in group_copies:
        copy.wait()
    all_copies = [
        send(scale_group, scale_ref.at[depth], all_send.at[k - 1], all_recv.at[k - 1],
             along_depth(k))
        for k in range(1, GROUP)
    ]
    for copy in all_copies:
        copy.start()
    scale_ref[depth] = scale_group[...]

    for k in range(1, GROUP):
        gc_copy(k).wait()
    gathered = context_out[depth].astype(jnp.float32)
    for k in range(1, GROUP):
        gathered = gathered + context_in[ahead(depth, GROUP - k)].astype(jnp.float32)
    grad_context_ref[...] = gathered.astype(jnp.bfloat16)
    for copy in all_copies:
        copy.wait()


def two_level(grad_rows, row_target, stored_context, block_scale, w_out, layer_scale):
    encoders = lax.axis_size("edata")
    owners = lax.axis_size("llm")
    source_rows, features = grad_rows.shape
    slot_count, columns = stored_context.shape
    capacity = slot_count // (encoders * owners)
    depth = lax.axis_index("edata") // GROUP
    share = features // encoders
    padded = up(share, 16)
    width = up(GROUP * padded, 128)
    block = GROUP * GROUP * capacity

    scaled = (grad_rows.astype(jnp.float32) * layer_scale[None, :]).astype(jnp.bfloat16)
    rows = jnp.pad(
        scaled.reshape(source_rows, encoders, share), ((0, 0), (0, 0), (0, padded - share))
    ).reshape(source_rows, GROUP, GROUP * padded)
    rows = jnp.pad(rows, ((0, 0), (0, 0), (0, width - GROUP * padded))).transpose(1, 0, 2)

    targets = row_target[:, 0]
    earlier = jnp.arange(source_rows)[None, :] < jnp.arange(source_rows)[:, None]
    same = targets[None, :] == targets[:, None]
    arrival = jnp.sum(jnp.where(earlier & same, 1, 0).astype(jnp.int32), axis=1)
    place = (
        (targets % GROUP) * block
        + ((targets // GROUP) * GROUP + depth) * capacity
        + arrival
    )
    lane = jnp.arange(GROUP * source_rows)
    place = jnp.where(lane // source_rows == depth, jnp.tile(place, GROUP), 0)
    place = jnp.broadcast_to(place[None, :], (8, GROUP * source_rows)).astype(jnp.int32)

    stored = stored_context.astype(jnp.float32).reshape(slot_count, -1, BLOCK)
    context = (stored * block_scale[:, :, None]).reshape(slot_count, -1).astype(jnp.bfloat16)
    weight = jnp.pad(w_out.T, ((0, padded - share), (0, 0)))
    rescale = 1.0 / math.sqrt(source_rows * encoders * owners)

    total = GROUP * slot_count
    bf16, f32 = jnp.bfloat16, jnp.float32
    small = up(padded, 128)
    sems = [3, 3, 3, 3, 3, 3, 3, 3, 7, 7, 3, 3, 3, 3, 1, 1, 3, 3, 3, 3]
    grad_context, grad_weight, scales = pl.pallas_call(
        functools.partial(kernel, capacity, rescale),
        out_shape=(
            jax.ShapeDtypeStruct((slot_count, columns), bf16),
            jax.ShapeDtypeStruct((share, columns), f32),
            jax.ShapeDtypeStruct((GROUP, GROUP, 8, small), f32),
        ),
        in_specs=[pl.BlockSpec(memory_space=pltpu.VMEM)] * 4,
        out_specs=[pl.BlockSpec(memory_space=pltpu.VMEM)] * 3,
        scratch_shapes=[
            pltpu.VMEM((GROUP, source_rows, width), bf16),
            pltpu.VMEM((GROUP, 8, GROUP * source_rows), jnp.int32),
            pltpu.VMEM((GROUP, block, width), bf16),
            pltpu.VMEM((owners * GROUP, block, width), bf16),
            pltpu.VMEM((GROUP, slot_count, width), bf16),
            pltpu.VMEM((GROUP, padded, total), bf16),
            pltpu.VMEM((GROUP, slot_count, columns), bf16),
            pltpu.VMEM((GROUP, padded, columns), bf16),
            pltpu.VMEM((GROUP, slot_count, columns), bf16),
            pltpu.VMEM((GROUP, slot_count, columns), bf16),
            pltpu.VMEM((GROUP, padded, columns), bf16),
            pltpu.VMEM((GROUP, padded, columns), bf16),
            pltpu.VMEM((2, 8, small), f32),
            pltpu.VMEM((GROUP, 8, small), f32),
        ]
        + [pltpu.SemaphoreType.DMA((n,)) for n in sems],
        compiler_params=pltpu.CompilerParams(
            collective_id=0, has_side_effects=True, vmem_limit_bytes=48 * 2**20
        ),
    )(rows, place, context, weight)
    grad_scale = scales[:, :, 0, :share].reshape(features) / layer_scale
    return (grad_context, grad_weight, grad_scale)


def on_device(grad_rows, row_target, stored_context, block_scale, w_out, layer_scale):
    encoders = lax.axis_size("edata")
    owners = lax.axis_size("llm")
    source_rows = grad_rows.shape[0]
    features = grad_rows.shape[1]
    slot_count = stored_context.shape[0]
    capacity = slot_count // (encoders * owners)
    weights = lax.all_gather(w_out, "edata", axis=1, tiled=True)
    targets = row_target[:, 0]
    chosen = (targets[:, None] == jnp.arange(encoders, dtype=jnp.int32)[None, :]).astype(jnp.int32)
    arrival = jnp.sum(chosen * (jnp.cumsum(chosen, axis=0) - 1), axis=1)
    position = targets * capacity + arrival
    outgoing = jnp.zeros((encoders * capacity, features), jnp.bfloat16).at[position].set(grad_rows)
    arrived = lax.all_to_all(outgoing, "edata", split_axis=0, concat_axis=0, tiled=True)
    grad_slots = lax.all_gather(arrived, "llm", axis=0, tiled=True)
    stored = stored_context.astype(jnp.float32).reshape(slot_count, -1, BLOCK)
    context = (stored * block_scale[:, :, None]).reshape(slot_count, -1).astype(jnp.bfloat16)
    scaled = (grad_slots.astype(jnp.float32) * layer_scale[None, :]).astype(jnp.bfloat16)
    recomputed = jnp.dot(context, weights, preferred_element_type=jnp.float32)
    grad_context = lax.dot_general(
        scaled, weights, (((1,), (1,)), ((), ())), preferred_element_type=jnp.float32
    ).astype(jnp.bfloat16)
    partial_scale = jnp.sum(grad_slots.astype(jnp.float32) * recomputed, axis=0)
    rescale = 1.0 / math.sqrt(source_rows * encoders * owners)
    grad_weight = (
        lax.psum_scatter(
            lax.dot_general(
                scaled, context, (((0,), (0,)), ((), ())), preferred_element_type=jnp.float32
            ),
            "edata",
            scatter_dimension=0,
            tiled=True,
        )
        * rescale
    )
    grad_scale = lax.psum(partial_scale, ("edata", "llm")) * rescale
    return (grad_context, grad_weight, grad_scale)


def solution(mesh):
    in_specs = (
        P(("edata", "llm"), None),
        P(("edata", "llm"), None),
        P("edata", "llm"),
        P("edata", "llm"),
        P("llm", "edata"),
        P(),
    )
    out_specs = (P("edata", "llm"), P("edata", "llm"), P())
    two_levels = mesh.shape["edata"] == GROUP * GROUP and mesh.shape["llm"] == 2
    return jax.shard_map(
        two_level if two_levels else on_device, mesh=mesh, in_specs=in_specs, out_specs=out_specs, check_vma=False
    )
```

```python
import functools
import math

import jax
import jax.numpy as jnp
from jax import lax
from jax.experimental import pallas as pl
from jax.experimental.pallas import tpu as pltpu
from jax.sharding import PartitionSpec as P

BLOCK = 128
GROUP = 4
MESH = pl.DeviceIdType.MESH


def up(value, unit):
    return -(-value // unit) * unit


def kernel(
    capacity, rescale, gradient_ref, target_ref, stored_ref, block_ref, weight_in_ref, layer_ref,
    grad_context_ref, grad_weight_ref, scale_ref,
    gradient, scaled, stored, row_buf, place_buf, routed, arrived, grads, grads_t, contexts,
    weights, context_own, up_out, up_in, down_out, down_in, weight_out, weight_in,
    scale_plane, scale_group,
    load_sem, row_send, row_recv, place_send, place_recv, weight_send, weight_recv,
    routed_send, routed_recv, cu_send, cu_recv, cd_send, cd_recv, gu_send, gu_recv,
    gd_send, gd_recv, gw_send, gw_recv, plane_send, plane_recv, all_send, all_recv,
):
    e, core = lax.axis_index("edata"), lax.axis_index("llm")
    depth, plane = e // GROUP, e % GROUP
    other = 1 - core
    last = GROUP - 1
    share = weight_in_ref.shape[0]
    features = weights.shape[1]
    slots = stored.shape[0]
    block = routed.shape[1]
    source_rows, width = row_buf.shape[1:]

    def ahead(own, k):
        return (own + k) % GROUP

    def along_depth(k):
        return (ahead(depth, k) * GROUP + plane, core)

    def along_plane(k, owner):
        return (depth * GROUP + ahead(plane, k), owner)

    def send(src, dst, send_sem, recv_sem, device):
        return pltpu.make_async_remote_copy(
            src_ref=src, dst_ref=dst, send_sem=send_sem, recv_sem=recv_sem,
            device_id=device, device_id_type=MESH,
        )

    loads = [
        pltpu.make_async_copy(gradient_ref, gradient, load_sem.at[0]),
        pltpu.make_async_copy(stored_ref, stored, load_sem.at[1]),
    ]
    for copy in loads:
        copy.start()
    barrier = pltpu.get_barrier_semaphore()
    for k in range(1, GROUP):
        pl.semaphore_signal(barrier, inc=1, device_id=along_depth(k), device_id_type=MESH)
        for owner in (core, other):
            pl.semaphore_signal(
                barrier, inc=1, device_id=along_plane(k, owner), device_id_type=MESH
            )
    pl.semaphore_signal(barrier, inc=1, device_id=(e, other), device_id_type=MESH)

    target = jnp.broadcast_to(target_ref[...], (source_rows, source_rows))
    first = lax.broadcasted_iota(jnp.int32, (source_rows, source_rows), 0)
    second = lax.broadcasted_iota(jnp.int32, (source_rows, source_rows), 1)
    column = target.astype(jnp.float32).T.astype(jnp.int32)
    before = jnp.where((target == column) & (first < second), 1.0, 0.0)
    arrival = jnp.sum(before, axis=0, keepdims=True).astype(jnp.int32)
    target = target_ref[...]
    place = (target & 3) * block + ((target >> 2) * GROUP + depth) * capacity + arrival
    spread = jnp.concatenate([place] * GROUP, axis=1)
    lane = lax.broadcasted_iota(jnp.int32, spread.shape, 1)
    begin = depth * source_rows
    inside = (lane >= begin) & (lane < begin + source_rows)
    place_buf[depth] = jnp.broadcast_to(jnp.where(inside, spread, 0), place_buf.shape[1:])
    weights[plane, :share, :] = weight_in_ref[...]
    weights[plane, share:, :] = jnp.zeros((features - share, weights.shape[2]), weights.dtype)
    loads[0].wait()
    scaled[...] = (gradient[...].astype(jnp.float32) * layer_ref[...]).astype(jnp.bfloat16)
    pl.semaphore_wait(barrier, 3 * last + 1)

    def window(at):
        return pl.multiple_of((at * (GROUP * share)) // BLOCK * BLOCK, BLOCK)

    row_copies = []
    place_copies = []
    for k in range(1, GROUP):
        row_copies.append(
            send(scaled.at[:, pl.ds(window(ahead(depth, k)), width)], row_buf.at[depth],
                 row_send.at[k - 1], row_recv.at[k - 1], along_depth(k))
        )
        place_copies.append(
            send(place_buf.at[depth], place_buf.at[depth],
                 place_send.at[k - 1], place_recv.at[k - 1], along_depth(k))
        )
    for copy in place_copies + row_copies:
        copy.start()
    weight_copies = [
        send(weights.at[plane], weights.at[plane], weight_send.at[k - 1], weight_recv.at[k - 1],
             along_plane(k, core))
        for k in range(1, GROUP)
    ]
    for copy in weight_copies:
        copy.start()
    row_buf[depth] = scaled[:, pl.ds(window(depth), width)]

    loads[1].wait()
    factors = block_ref[...].T
    for j in range(factors.shape[1]):
        part = slice(j * BLOCK, (j + 1) * BLOCK)
        contexts[depth, :, part] = (
            stored[:, part].astype(jnp.float32) * factors[:, j : j + 1]
        ).astype(jnp.bfloat16)

    def context_up(s):
        return send(contexts.at[depth - s], contexts.at[depth - s], cu_send.at[s],
                    cu_recv.at[s], ((depth + 1) * GROUP + plane, core))

    def context_down(s):
        return send(contexts.at[depth + s], contexts.at[depth + s], cd_send.at[s],
                    cd_recv.at[s], ((depth - 1) * GROUP + plane, core))

    def context_wait(s):
        @pl.when(depth - 1 - s >= 0)
        def _():
            below = contexts.at[depth - 1 - s]
            send(below, below, cu_send.at[s], cu_recv.at[s], (e, other)).wait_recv()

        @pl.when(depth + 1 + s <= last)
        def _():
            above = contexts.at[depth + 1 + s]
            send(above, above, cd_send.at[s], cd_recv.at[s], (e, other)).wait_recv()

    def context_step(s):
        if s > 0:
            context_wait(s - 1)

        @pl.when((depth < last) & (depth - s >= 0))
        def _():
            context_up(s).start()

        @pl.when((depth > 0) & (depth + s <= last))
        def _():
            context_down(s).start()

    lane = lax.broadcasted_iota(jnp.int32, (1, GROUP * features), 1)
    part = jnp.zeros_like(lane)
    for k in range(1, GROUP):
        part = part + jnp.where(lane >= k * features, 1, 0)
    within = lane - part * features
    source = depth * (GROUP * share) - window(depth) + part * share + within
    source = jnp.where(within < share, source, -1)
    select = jnp.where(
        lax.broadcasted_iota(jnp.int32, (width, GROUP * features), 0) == source, 1.0, 0.0
    ).astype(jnp.bfloat16)

    for copy in place_copies:
        copy.wait()
    places = place_buf[0, 0:1, :]
    for j in range(1, GROUP):
        places = places + place_buf[j, 0:1, :]
    wanted = lax.broadcasted_iota(jnp.int32, (GROUP * block, GROUP * source_rows), 0)
    choice = jnp.where(wanted == places, 1.0, 0.0).astype(jnp.bfloat16)
    for copy in row_copies:
        copy.wait()
    context_step(0)
    owned = jnp.dot(
        row_buf[...].reshape(GROUP * source_rows, width), select,
        preferred_element_type=jnp.float32,
    ).astype(jnp.bfloat16)
    routed[...] = (
        jnp.dot(choice, owned, preferred_element_type=jnp.float32)
        .astype(jnp.bfloat16)
        .reshape(GROUP, block, GROUP * features)
    )
    mine = core * GROUP + plane
    routed_copies = []
    for k in range(1, GROUP):
        for which, owner in enumerate((core, other)):
            index = 2 * (k - 1) + which
            routed_copies.append(
                send(routed.at[ahead(plane, k)], arrived.at[mine],
                     routed_send.at[index], routed_recv.at[index], along_plane(k, owner))
            )
    routed_copies.append(
        send(routed.at[plane], arrived.at[mine], routed_send.at[2 * last],
             routed_recv.at[2 * last], (e, other))
    )
    for copy in routed_copies:
        copy.start()
    arrived[mine] = routed[plane]
    context_step(1)

    total = GROUP * slots
    slot = lax.broadcasted_iota(jnp.int32, (total, 1), 0)
    fifth = (slot * (2**18 // capacity + 1)) >> 18
    found_arrival = slot - fifth * capacity
    plane_of, source_depth = fifth & 3, (fifth >> 2) & 3
    core_of, target_depth = (fifth >> 4) & 1, fifth >> 5
    found = (
        (core_of * GROUP + plane_of) * block
        + (target_depth * GROUP + source_depth) * capacity
        + found_arrival
    )
    order = jnp.where(
        lax.broadcasted_iota(jnp.int32, (total, total), 1) == found, 1.0, 0.0
    ).astype(jnp.bfloat16)
    context_step(2)
    for copy in routed_copies:
        copy.wait()
    ordered = jnp.dot(
        order, arrived[...].reshape(total, GROUP * features), preferred_element_type=jnp.float32
    )
    grads[...] = ordered.astype(jnp.bfloat16).reshape(GROUP, slots, GROUP * features)
    grads_t[...] = ordered.T.astype(jnp.bfloat16).reshape(GROUP, features, total)

    for copy in weight_copies:
        copy.wait()

    def own_step(k, carry):
        at = (depth + 2 + k) % GROUP
        context_own[at] = jnp.dot(
            grads[at], weights[...].reshape(GROUP * features, -1),
            preferred_element_type=jnp.float32,
        )
        return carry

    lax.fori_loop(0, GROUP, own_step, 0)

    def sum_up(s):
        return send(up_out.at[s], up_in.at[s], gu_send.at[s], gu_recv.at[s],
                    ((depth + 1) * GROUP + plane, core))

    def sum_down(s):
        return send(down_out.at[s], down_in.at[s], gd_send.at[s], gd_recv.at[s],
                    ((depth - 1) * GROUP + plane, core))

    def up_wait(s):
        send(up_in.at[s], up_in.at[s], gu_send.at[s], gu_recv.at[s], (e, other)).wait_recv()

    def down_wait(s):
        send(down_in.at[s], down_in.at[s], gd_send.at[s], gd_recv.at[s], (e, other)).wait_recv()

    def sum_step(s):
        @pl.when((depth < last) & (depth <= s))
        def _():
            at = last + depth - s
            if s == 0:
                up_out[s] = context_own[at].astype(jnp.bfloat16)
            else:

                @pl.when(depth == 0)
                def _():
                    up_out[s] = context_own[at].astype(jnp.bfloat16)

                @pl.when(depth > 0)
                def _():
                    up_wait(s - 1)
                    up_out[s] = (
                        context_own[at] + up_in[s - 1].astype(jnp.float32)
                    ).astype(jnp.bfloat16)

            sum_up(s).start()

        @pl.when((depth > 0) & (last - depth <= s))
        def _():
            at = depth - last + s
            if s == 0:
                down_out[s] = context_own[at].astype(jnp.bfloat16)
            else:

                @pl.when(depth == last)
                def _():
                    down_out[s] = context_own[at].astype(jnp.bfloat16)

                @pl.when(depth < last)
                def _():
                    down_wait(s - 1)
                    down_out[s] = (
                        context_own[at] + down_in[s - 1].astype(jnp.float32)
                    ).astype(jnp.bfloat16)

            sum_down(s).start()

    sum_step(0)

    context_wait(2)

    def gw_copy(k):
        return send(weight_out.at[ahead(plane, k)], weight_in.at[plane],
                    gw_send.at[k - 1], gw_recv.at[k - 1], along_plane(k, core))

    def weight_step(k, carry):
        at = ahead(plane, k)
        weight_out[at] = jnp.dot(
            grads_t[at], contexts[...].reshape(total, -1), preferred_element_type=jnp.float32
        ).astype(jnp.bfloat16)

        @pl.when(k < GROUP)
        def _():
            gw_copy(k).start()

        return carry

    lax.fori_loop(1, GROUP + 1, weight_step, 0)
    sum_step(1)
    sum_step(2)

    for k in range(1, GROUP):
        gw_copy(k).wait()
    summed = weight_out[plane].astype(jnp.float32)
    for k in range(1, GROUP):
        summed = summed + weight_in[ahead(plane, GROUP - k)].astype(jnp.float32)
    product = summed * weights[plane].astype(jnp.float32)
    lanes = product[:, :BLOCK]
    for j in range(1, product.shape[1] // BLOCK):
        lanes = lanes + product[:, j * BLOCK : (j + 1) * BLOCK]
    own = jnp.sum(lanes.T, axis=0, keepdims=True) * rescale
    pad = scale_plane.shape[2] - features
    own = jnp.broadcast_to(jnp.pad(own, ((0, 0), (0, pad))), scale_plane.shape[1:])

    scale_plane[mine] = own
    plane_copies = []
    for k in range(GROUP):
        for which, owner in enumerate((other, core)):
            if k > 0 or which == 0:
                index = 2 * k + which - (1 if k > 0 else 0)
                plane_copies.append(
                    send(scale_plane.at[mine], scale_plane.at[mine], plane_send.at[index],
                         plane_recv.at[index], along_plane(k, owner))
                )
    for copy in plane_copies:
        copy.start()
    grad_weight_ref[...] = summed[:share, :] * rescale
    for copy in plane_copies:
        copy.wait()
    for j in range(GROUP):
        scale_group[j] = scale_plane[j] + scale_plane[GROUP + j]
    all_copies = [
        send(scale_group, scale_ref.at[depth], all_send.at[k - 1], all_recv.at[k - 1],
             along_depth(k))
        for k in range(1, GROUP)
    ]
    for copy in all_copies:
        copy.start()
    scale_ref[depth] = scale_group[...]

    @pl.when(depth > 0)
    def _():
        up_wait(2)
        context_own[depth] += up_in[2].astype(jnp.float32)

    @pl.when(depth < last)
    def _():
        down_wait(2)
        context_own[depth] += down_in[2].astype(jnp.float32)

    grad_context_ref[...] = context_own[depth].astype(jnp.bfloat16)

    for s in range(last):

        @pl.when((depth < last) & (depth - s >= 0))
        def _():
            context_up(s).wait_send()

        @pl.when((depth > 0) & (depth + s <= last))
        def _():
            context_down(s).wait_send()

        @pl.when((depth < last) & (depth <= s))
        def _():
            sum_up(s).wait_send()

        @pl.when((depth > 0) & (last - depth <= s))
        def _():
            sum_down(s).wait_send()

    for copy in all_copies:
        copy.wait()


def two_level(grad_rows, row_target, stored_context, block_scale, w_out, layer_scale):
    encoders = lax.axis_size("edata")
    owners = lax.axis_size("llm")
    source_rows, features = grad_rows.shape
    slot_count, columns = stored_context.shape
    capacity = slot_count // (encoders * owners)
    share = features // encoders
    padded = up(share, 16)
    starts = [d * GROUP * share // BLOCK * BLOCK for d in range(GROUP)]
    width = max(up((d + 1) * GROUP * share, BLOCK) - starts[d] for d in range(GROUP))
    block = GROUP * GROUP * capacity
    rescale = 1.0 / math.sqrt(source_rows * encoders * owners)

    total = GROUP * slot_count
    bf16, f32 = jnp.bfloat16, jnp.float32
    small = up(padded, 128)
    sems = [2, 3, 3, 3, 3, 3, 3, 7, 7, 3, 3, 3, 3, 3, 3, 3, 3, 3, 3, 7, 7, 3, 3]
    vmem = pl.BlockSpec(memory_space=pltpu.VMEM)
    far = pl.BlockSpec(memory_space=pl.ANY)
    grad_context, grad_weight, scales = pl.pallas_call(
        functools.partial(kernel, capacity, rescale),
        out_shape=(
            jax.ShapeDtypeStruct((slot_count, columns), bf16),
            jax.ShapeDtypeStruct((share, columns), f32),
            jax.ShapeDtypeStruct((GROUP, GROUP, 8, small), f32),
        ),
        in_specs=[far, vmem, far, vmem, vmem, vmem],
        out_specs=[vmem] * 3,
        scratch_shapes=[
            pltpu.VMEM((source_rows, features), bf16),
            pltpu.VMEM((source_rows, features), bf16),
            pltpu.VMEM((slot_count, columns), bf16),
            pltpu.VMEM((GROUP, source_rows, width), bf16),
            pltpu.VMEM((GROUP, 8, GROUP * source_rows), jnp.int32),
            pltpu.VMEM((GROUP, block, GROUP * padded), bf16),
            pltpu.VMEM((owners * GROUP, block, GROUP * padded), bf16),
            pltpu.VMEM((GROUP, slot_count, GROUP * padded), bf16),
            pltpu.VMEM((GROUP, padded, total), bf16),
            pltpu.VMEM((GROUP, slot_count, columns), bf16),
            pltpu.VMEM((GROUP, padded, columns), bf16),
            pltpu.VMEM((GROUP, slot_count, columns), f32),
            pltpu.VMEM((GROUP - 1, slot_count, columns), bf16),
            pltpu.VMEM((GROUP - 1, slot_count, columns), bf16),
            pltpu.VMEM((GROUP - 1, slot_count, columns), bf16),
            pltpu.VMEM((GROUP - 1, slot_count, columns), bf16),
            pltpu.VMEM((GROUP, padded, columns), bf16),
            pltpu.VMEM((GROUP, padded, columns), bf16),
            pltpu.VMEM((owners * GROUP, 8, small), f32),
            pltpu.VMEM((GROUP, 8, small), f32),
        ]
        + [pltpu.SemaphoreType.DMA((n,)) for n in sems],
        compiler_params=pltpu.CompilerParams(
            collective_id=0, has_side_effects=True, vmem_limit_bytes=48 * 2**20
        ),
    )(grad_rows, row_target.T, stored_context, block_scale.T, w_out.T, layer_scale[None, :])
    grad_scale = scales[:, :, 0, :share].reshape(features) / layer_scale
    return (grad_context, grad_weight, grad_scale)


def on_device(grad_rows, row_target, stored_context, block_scale, w_out, layer_scale):
    encoders = lax.axis_size("edata")
    owners = lax.axis_size("llm")
    source_rows = grad_rows.shape[0]
    features = grad_rows.shape[1]
    slot_count = stored_context.shape[0]
    capacity = slot_count // (encoders * owners)
    weights = lax.all_gather(w_out, "edata", axis=1, tiled=True)
    targets = row_target[:, 0]
    chosen = (targets[:, None] == jnp.arange(encoders, dtype=jnp.int32)[None, :]).astype(jnp.int32)
    arrival = jnp.sum(chosen * (jnp.cumsum(chosen, axis=0) - 1), axis=1)
    position = targets * capacity + arrival
    outgoing = jnp.zeros((encoders * capacity, features), jnp.bfloat16).at[position].set(grad_rows)
    arrived = lax.all_to_all(outgoing, "edata", split_axis=0, concat_axis=0, tiled=True)
    grad_slots = lax.all_gather(arrived, "llm", axis=0, tiled=True)
    stored = stored_context.astype(jnp.float32).reshape(slot_count, -1, BLOCK)
    context = (stored * block_scale[:, :, None]).reshape(slot_count, -1).astype(jnp.bfloat16)
    scaled = (grad_slots.astype(jnp.float32) * layer_scale[None, :]).astype(jnp.bfloat16)
    recomputed = jnp.dot(context, weights, preferred_element_type=jnp.float32)
    grad_context = lax.dot_general(
        scaled, weights, (((1,), (1,)), ((), ())), preferred_element_type=jnp.float32
    ).astype(jnp.bfloat16)
    partial_scale = jnp.sum(grad_slots.astype(jnp.float32) * recomputed, axis=0)
    rescale = 1.0 / math.sqrt(source_rows * encoders * owners)
    grad_weight = (
        lax.psum_scatter(
            lax.dot_general(
                scaled, context, (((0,), (0,)), ((), ())), preferred_element_type=jnp.float32
            ),
            "edata",
            scatter_dimension=0,
            tiled=True,
        )
        * rescale
    )
    grad_scale = lax.psum(partial_scale, ("edata", "llm")) * rescale
    return (grad_context, grad_weight, grad_scale)


def solution(mesh):
    in_specs = (
        P(("edata", "llm"), None),
        P(("edata", "llm"), None),
        P("edata", "llm"),
        P("edata", "llm"),
        P("llm", "edata"),
        P(),
    )
    out_specs = (P("edata", "llm"), P("edata", "llm"), P())
    two_levels = mesh.shape["edata"] == GROUP * GROUP and mesh.shape["llm"] == 2
    return jax.shard_map(
        two_level if two_levels else on_device, mesh=mesh, in_specs=in_specs, out_specs=out_specs, check_vma=False
    )
```

```python
import functools
import math

import jax
import jax.numpy as jnp
from jax import lax
from jax.experimental import pallas as pl
from jax.experimental.pallas import tpu as pltpu
from jax.sharding import PartitionSpec as P

BLOCK = 128
GROUP = 4
MESH = pl.DeviceIdType.MESH


def up(value, unit):
    return -(-value // unit) * unit


def kernel(
    capacity, rescale, gradient_ref, target_ref, stored_ref, block_ref, weight_in_ref, layer_in_ref,
    grad_context_ref, grad_weight_ref, scale_ref,
    gradient, scaled, stored, targets, blocks, weight_own, layer, row_buf, place_buf, routed, arrived, grads, grads_t, contexts,
    weights, context_own, up_out, up_in, down_out, down_in, weight_out, weight_in,
    scale_plane, scale_group,
    load_sem, row_send, row_recv, place_send, place_recv, weight_send, weight_recv,
    routed_send, routed_recv, cu_send, cu_recv, cd_send, cd_recv, gu_send, gu_recv,
    gd_send, gd_recv, gw_send, gw_recv, plane_send, plane_recv, all_send, all_recv,
):
    e, core = lax.axis_index("edata"), lax.axis_index("llm")
    depth, plane = e // GROUP, e % GROUP
    other = 1 - core
    last = GROUP - 1
    share = weight_own.shape[0]
    features = weights.shape[1]
    slots = stored.shape[0]
    block = routed.shape[1]
    source_rows, width = row_buf.shape[1:]

    def ahead(own, k):
        return (own + k) % GROUP

    def along_depth(k):
        return (ahead(depth, k) * GROUP + plane, core)

    def along_plane(k, owner):
        return (depth * GROUP + ahead(plane, k), owner)

    def send(src, dst, send_sem, recv_sem, device):
        return pltpu.make_async_remote_copy(
            src_ref=src, dst_ref=dst, send_sem=send_sem, recv_sem=recv_sem,
            device_id=device, device_id_type=MESH,
        )

    loads = [
        pltpu.make_async_copy(gradient_ref, gradient, load_sem.at[0]),
        pltpu.make_async_copy(layer_in_ref, layer, load_sem.at[1]),
        pltpu.make_async_copy(target_ref, targets, load_sem.at[2]),
        pltpu.make_async_copy(weight_in_ref, weight_own, load_sem.at[3]),
        pltpu.make_async_copy(stored_ref, stored, load_sem.at[4]),
        pltpu.make_async_copy(block_ref, blocks, load_sem.at[5]),
    ]
    for copy in loads:
        copy.start()
    barrier = pltpu.get_barrier_semaphore()
    for k in range(1, GROUP):
        pl.semaphore_signal(barrier, inc=1, device_id=along_depth(k), device_id_type=MESH)
        for owner in (core, other):
            pl.semaphore_signal(
                barrier, inc=1, device_id=along_plane(k, owner), device_id_type=MESH
            )
    pl.semaphore_signal(barrier, inc=1, device_id=(e, other), device_id_type=MESH)

    loads[2].wait()
    target = jnp.broadcast_to(targets[...], (source_rows, source_rows))
    first = lax.broadcasted_iota(jnp.int32, (source_rows, source_rows), 0)
    second = lax.broadcasted_iota(jnp.int32, (source_rows, source_rows), 1)
    column = target.astype(jnp.float32).T.astype(jnp.int32)
    before = jnp.where((target == column) & (first < second), 1.0, 0.0)
    arrival = jnp.sum(before, axis=0, keepdims=True).astype(jnp.int32)
    target = targets[...]
    place = (target & 3) * block + ((target >> 2) * GROUP + depth) * capacity + arrival
    spread = jnp.concatenate([place] * GROUP, axis=1)
    lane = lax.broadcasted_iota(jnp.int32, spread.shape, 1)
    begin = depth * source_rows
    inside = (lane >= begin) & (lane < begin + source_rows)
    place_buf[depth] = jnp.broadcast_to(jnp.where(inside, spread, 0), place_buf.shape[1:])
    loads[3].wait()
    weights[plane, :share, :] = weight_own[...]
    weights[plane, share:, :] = jnp.zeros((features - share, weights.shape[2]), weights.dtype)
    loads[0].wait()
    loads[1].wait()
    scaled[...] = (gradient[...].astype(jnp.float32) * layer[...].reshape(1, -1)).astype(jnp.bfloat16)
    pl.semaphore_wait(barrier, 3 * last + 1)

    def window(at):
        return pl.multiple_of((at * (GROUP * share)) // BLOCK * BLOCK, BLOCK)

    row_copies = []
    place_copies = []
    for k in range(1, GROUP):
        row_copies.append(
            send(scaled.at[:, pl.ds(window(ahead(depth, k)), width)], row_buf.at[depth],
                 row_send.at[k - 1], row_recv.at[k - 1], along_depth(k))
        )
        place_copies.append(
            send(place_buf.at[depth], place_buf.at[depth],
                 place_send.at[k - 1], place_recv.at[k - 1], along_depth(k))
        )
    for copy in place_copies + row_copies:
        copy.start()
    half = weights.shape[2] // 2
    beside = plane // 2 * 2 + (1 - plane % 2)
    across = (1 - plane // 2) * 2 + plane % 2

    def weight_copy(index, owner, part, to):
        ref = weights.at[owner, :, pl.ds(part * half, half)]
        return send(ref, ref, weight_send.at[index], weight_recv.at[index],
                    (depth * GROUP + to, core))

    weight_copies = [
        weight_copy(0, plane, 0, beside),
        weight_copy(1, plane, 1, across),
        weight_copy(2, plane, 1, beside),
        weight_copy(3, plane, 0, across),
    ]
    for copy in weight_copies:
        copy.start()
    row_buf[depth] = scaled[:, pl.ds(window(depth), width)]

    loads[4].wait()
    loads[5].wait()
    factors = blocks[...].T
    for j in range(factors.shape[1]):
        part = slice(j * BLOCK, (j + 1) * BLOCK)
        contexts[depth, :, part] = (
            stored[:, part].astype(jnp.float32) * factors[:, j : j + 1]
        ).astype(jnp.bfloat16)

    def context_up(s):
        return send(contexts.at[depth - s], contexts.at[depth - s], cu_send.at[s],
                    cu_recv.at[s], ((depth + 1) * GROUP + plane, core))

    def context_down(s):
        return send(contexts.at[depth + s], contexts.at[depth + s], cd_send.at[s],
                    cd_recv.at[s], ((depth - 1) * GROUP + plane, core))

    def context_wait(s):
        @pl.when(depth - 1 - s >= 0)
        def _():
            below = contexts.at[depth - 1 - s]
            send(below, below, cu_send.at[s], cu_recv.at[s], (e, other)).wait_recv()

        @pl.when(depth + 1 + s <= last)
        def _():
            above = contexts.at[depth + 1 + s]
            send(above, above, cd_send.at[s], cd_recv.at[s], (e, other)).wait_recv()

    def context_step(s):
        if s > 0:
            context_wait(s - 1)

        @pl.when((depth < last) & (depth - s >= 0))
        def _():
            context_up(s).start()

        @pl.when((depth > 0) & (depth + s <= last))
        def _():
            context_down(s).start()

    context_step(0)

    lane = lax.broadcasted_iota(jnp.int32, (1, GROUP * features), 1)
    part = jnp.zeros_like(lane)
    for k in range(1, GROUP):
        part = part + jnp.where(lane >= k * features, 1, 0)
    within = lane - part * features
    source = depth * (GROUP * share) - window(depth) + part * share + within
    source = jnp.where(within < share, source, -1)
    select = jnp.where(
        lax.broadcasted_iota(jnp.int32, (width, GROUP * features), 0) == source, 1.0, 0.0
    ).astype(jnp.bfloat16)

    total = GROUP * slots
    slot = lax.broadcasted_iota(jnp.int32, (total, 1), 0)
    fifth = (slot * (2**18 // capacity + 1)) >> 18
    found_arrival = slot - fifth * capacity
    plane_of, source_depth = fifth & 3, (fifth >> 2) & 3
    core_of, target_depth = (fifth >> 4) & 1, fifth >> 5
    found = (
        (core_of * GROUP + plane_of) * block
        + (target_depth * GROUP + source_depth) * capacity
        + found_arrival
    )
    order = jnp.where(
        lax.broadcasted_iota(jnp.int32, (total, total), 1) == found, 1.0, 0.0
    ).astype(jnp.bfloat16)
    for copy in place_copies:
        copy.wait()
    places = place_buf[0, 0:1, :]
    for j in range(1, GROUP):
        places = places + place_buf[j, 0:1, :]
    wanted = lax.broadcasted_iota(jnp.int32, (GROUP * block, GROUP * source_rows), 0)
    choice = jnp.where(wanted == places, 1.0, 0.0).astype(jnp.bfloat16)
    for copy in row_copies:
        copy.wait()
    owned = jnp.dot(
        row_buf[...].reshape(GROUP * source_rows, width), select,
        preferred_element_type=jnp.float32,
    ).astype(jnp.bfloat16)
    routed[...] = (
        jnp.dot(choice, owned, preferred_element_type=jnp.float32)
        .astype(jnp.bfloat16)
        .reshape(GROUP, block, GROUP * features)
    )
    mine = core * GROUP + plane
    routed_copies = []
    for k in range(1, GROUP):
        for which, owner in enumerate((core, other)):
            index = 2 * (k - 1) + which
            routed_copies.append(
                send(routed.at[ahead(plane, k)], arrived.at[mine],
                     routed_send.at[index], routed_recv.at[index], along_plane(k, owner))
            )
    routed_copies.append(
        send(routed.at[plane], arrived.at[mine], routed_send.at[2 * last],
             routed_recv.at[2 * last], (e, other))
    )
    for copy in routed_copies:
        copy.start()
    arrived[mine] = routed[plane]
    weight_copies[0].wait_recv()
    weight_copies[1].wait_recv()
    passed = [weight_copy(4, beside, 0, across), weight_copy(5, across, 1, beside)]
    for copy in passed:
        copy.start()
    context_step(1)
    context_step(2)
    for copy in routed_copies:
        copy.wait()
    ordered = jnp.dot(
        order, arrived[...].reshape(total, GROUP * features), preferred_element_type=jnp.float32
    )
    grads[...] = ordered.astype(jnp.bfloat16).reshape(GROUP, slots, GROUP * features)
    grads_t[...] = ordered.T.astype(jnp.bfloat16).reshape(GROUP, features, total)

    for copy in weight_copies[2:] + passed:
        copy.wait()
    for copy in weight_copies[:2]:
        copy.wait_send()
    upper = depth // (GROUP // 2)

    def own_step(k, carry):
        at = upper * k + (1 - upper) * (last - k)
        context_own[at] = jnp.dot(
            grads[at], weights[...].reshape(GROUP * features, -1),
            preferred_element_type=jnp.float32,
        )
        return carry


    part_rows = slots // 2

    def sum_up(s, h):
        return send(up_out.at[s, h], up_in.at[s, h], gu_send.at[2 * s + h], gu_recv.at[2 * s + h],
                    ((depth + 1) * GROUP + plane, core))

    def sum_down(s, h):
        return send(down_out.at[s, h], down_in.at[s, h], gd_send.at[2 * s + h],
                    gd_recv.at[2 * s + h], ((depth - 1) * GROUP + plane, core))

    def up_wait(s, h):
        ref = up_in.at[s, h]
        send(ref, ref, gu_send.at[2 * s + h], gu_recv.at[2 * s + h], (e, other)).wait_recv()

    def down_wait(s, h):
        ref = down_in.at[s, h]
        send(ref, ref, gd_send.at[2 * s + h], gd_recv.at[2 * s + h], (e, other)).wait_recv()

    def sum_step(s, h):
        piece = slice(h * part_rows, (h + 1) * part_rows)

        @pl.when((depth < last) & (depth <= s))
        def _():
            at = last + depth - s
            if s == 0:
                up_out[s, h] = context_own[at, piece].astype(jnp.bfloat16)
            else:

                @pl.when(depth == 0)
                def _():
                    up_out[s, h] = context_own[at, piece].astype(jnp.bfloat16)

                @pl.when(depth > 0)
                def _():
                    up_wait(s - 1, h)
                    up_out[s, h] = (
                        context_own[at, piece] + up_in[s - 1, h].astype(jnp.float32)
                    ).astype(jnp.bfloat16)

            sum_up(s, h).start()

        @pl.when((depth > 0) & (last - depth <= s))
        def _():
            at = depth - last + s
            if s == 0:
                down_out[s, h] = context_own[at, piece].astype(jnp.bfloat16)
            else:

                @pl.when(depth == last)
                def _():
                    down_out[s, h] = context_own[at, piece].astype(jnp.bfloat16)

                @pl.when(depth < last)
                def _():
                    down_wait(s - 1, h)
                    down_out[s, h] = (
                        context_own[at, piece] + down_in[s - 1, h].astype(jnp.float32)
                    ).astype(jnp.bfloat16)

            sum_down(s, h).start()

    own_step(0, 0)
    sum_step(0, 0)
    sum_step(0, 1)
    lax.fori_loop(1, GROUP, own_step, 0)

    context_wait(2)

    def gw_copy(k):
        return send(weight_out.at[ahead(plane, k)], weight_in.at[plane],
                    gw_send.at[k - 1], gw_recv.at[k - 1], along_plane(k, core))

    def weight_step(k, carry):
        at = ahead(plane, k)
        weight_out[at] = jnp.dot(
            grads_t[at], contexts[...].reshape(total, -1), preferred_element_type=jnp.float32
        ).astype(jnp.bfloat16)

        @pl.when(k < GROUP)
        def _():
            gw_copy(k).start()

        return carry

    lax.fori_loop(1, GROUP + 1, weight_step, 0)
    for s in range(1, last):
        for h in range(2):
            sum_step(s, h)

    for k in range(1, GROUP):
        gw_copy(k).wait()
    summed = weight_out[plane].astype(jnp.float32)
    for k in range(1, GROUP):
        summed = summed + weight_in[ahead(plane, GROUP - k)].astype(jnp.float32)
    product = summed * weights[plane].astype(jnp.float32)
    lanes = product[:, :BLOCK]
    for j in range(1, product.shape[1] // BLOCK):
        lanes = lanes + product[:, j * BLOCK : (j + 1) * BLOCK]
    own = jnp.sum(lanes.T, axis=0, keepdims=True) * rescale
    pad = scale_plane.shape[2] - features
    own = jnp.broadcast_to(jnp.pad(own, ((0, 0), (0, pad))), scale_plane.shape[1:])

    scale_plane[mine] = own
    plane_copies = []
    for k in range(GROUP):
        for which, owner in enumerate((other, core)):
            if k > 0 or which == 0:
                index = 2 * k + which - (1 if k > 0 else 0)
                plane_copies.append(
                    send(scale_plane.at[mine], scale_plane.at[mine], plane_send.at[index],
                         plane_recv.at[index], along_plane(k, owner))
                )
    for copy in plane_copies:
        copy.start()
    grad_weight_ref[...] = summed[:share, :] * rescale
    for copy in plane_copies:
        copy.wait()
    for j in range(GROUP):
        scale_group[j] = scale_plane[j] + scale_plane[GROUP + j]
    all_copies = [
        send(scale_group, scale_ref.at[depth], all_send.at[k - 1], all_recv.at[k - 1],
             along_depth(k))
        for k in range(1, GROUP)
    ]
    for copy in all_copies:
        copy.start()
    scale_ref[depth] = scale_group[...]

    for h in range(2):
        piece = slice(h * part_rows, (h + 1) * part_rows)

        @pl.when(depth > 0)
        def _():
            up_wait(last - 1, h)
            context_own[depth, piece] += up_in[last - 1, h].astype(jnp.float32)

        @pl.when(depth < last)
        def _():
            down_wait(last - 1, h)
            context_own[depth, piece] += down_in[last - 1, h].astype(jnp.float32)

        grad_context_ref[piece, :] = context_own[depth, piece].astype(jnp.bfloat16)

    for s in range(last):

        @pl.when((depth < last) & (depth - s >= 0))
        def _():
            context_up(s).wait_send()

        @pl.when((depth > 0) & (depth + s <= last))
        def _():
            context_down(s).wait_send()

        @pl.when((depth < last) & (depth <= s))
        def _():
            for h in range(2):
                sum_up(s, h).wait_send()

        @pl.when((depth > 0) & (last - depth <= s))
        def _():
            for h in range(2):
                sum_down(s, h).wait_send()

    for copy in all_copies:
        copy.wait()


def two_level(grad_rows, row_target, stored_context, block_scale, w_out, layer_scale):
    encoders = lax.axis_size("edata")
    owners = lax.axis_size("llm")
    source_rows, features = grad_rows.shape
    slot_count, columns = stored_context.shape
    capacity = slot_count // (encoders * owners)
    share = features // encoders
    padded = up(share, 16)
    starts = [d * GROUP * share // BLOCK * BLOCK for d in range(GROUP)]
    width = max(up((d + 1) * GROUP * share, BLOCK) - starts[d] for d in range(GROUP))
    block = GROUP * GROUP * capacity
    rescale = 1.0 / math.sqrt(source_rows * encoders * owners)

    total = GROUP * slot_count
    bf16, f32 = jnp.bfloat16, jnp.float32
    small = up(padded, 128)
    sems = [6, 3, 3, 3, 3, 6, 6, 7, 7, 3, 3, 3, 3, 6, 6, 6, 6, 3, 3, 7, 7, 3, 3]
    vmem = pl.BlockSpec(memory_space=pltpu.VMEM)
    far = pl.BlockSpec(memory_space=pltpu.HBM)
    grad_context, grad_weight, scales = pl.pallas_call(
        functools.partial(kernel, capacity, rescale),
        out_shape=(
            jax.ShapeDtypeStruct((slot_count, columns), bf16),
            jax.ShapeDtypeStruct((share, columns), f32),
            jax.ShapeDtypeStruct((GROUP, GROUP, 8, small), f32),
        ),
        in_specs=[far] * 6,
        out_specs=[vmem] * 3,
        scratch_shapes=[
            pltpu.VMEM((source_rows, features), bf16),
            pltpu.VMEM((source_rows, features), bf16),
            pltpu.VMEM((slot_count, columns), bf16),
            pltpu.VMEM((1, source_rows), jnp.int32),
            pltpu.VMEM((columns // BLOCK, slot_count), f32),
            pltpu.VMEM((share, columns), bf16),
            pltpu.VMEM((features,), f32),
            pltpu.VMEM((GROUP, source_rows, width), bf16),
            pltpu.VMEM((GROUP, 8, GROUP * source_rows), jnp.int32),
            pltpu.VMEM((GROUP, block, GROUP * padded), bf16),
            pltpu.VMEM((owners * GROUP, block, GROUP * padded), bf16),
            pltpu.VMEM((GROUP, slot_count, GROUP * padded), bf16),
            pltpu.VMEM((GROUP, padded, total), bf16),
            pltpu.VMEM((GROUP, slot_count, columns), bf16),
            pltpu.VMEM((GROUP, padded, columns), bf16),
            pltpu.VMEM((GROUP, slot_count, columns), f32),
            pltpu.VMEM((GROUP - 1, 2, slot_count // 2, columns), bf16),
            pltpu.VMEM((GROUP - 1, 2, slot_count // 2, columns), bf16),
            pltpu.VMEM((GROUP - 1, 2, slot_count // 2, columns), bf16),
            pltpu.VMEM((GROUP - 1, 2, slot_count // 2, columns), bf16),
            pltpu.VMEM((GROUP, padded, columns), bf16),
            pltpu.VMEM((GROUP, padded, columns), bf16),
            pltpu.VMEM((owners * GROUP, 8, small), f32),
            pltpu.VMEM((GROUP, 8, small), f32),
        ]
        + [pltpu.SemaphoreType.DMA((n,)) for n in sems],
        compiler_params=pltpu.CompilerParams(
            collective_id=0, has_side_effects=True, vmem_limit_bytes=64 * 2**20
        ),
    )(grad_rows, row_target.T, stored_context, block_scale.T, w_out.T, layer_scale)
    grad_scale = scales[:, :, 0, :share].reshape(features) / layer_scale
    return (grad_context, grad_weight, grad_scale)


def on_device(grad_rows, row_target, stored_context, block_scale, w_out, layer_scale):
    encoders = lax.axis_size("edata")
    owners = lax.axis_size("llm")
    source_rows = grad_rows.shape[0]
    features = grad_rows.shape[1]
    slot_count = stored_context.shape[0]
    capacity = slot_count // (encoders * owners)
    weights = lax.all_gather(w_out, "edata", axis=1, tiled=True)
    targets = row_target[:, 0]
    chosen = (targets[:, None] == jnp.arange(encoders, dtype=jnp.int32)[None, :]).astype(jnp.int32)
    arrival = jnp.sum(chosen * (jnp.cumsum(chosen, axis=0) - 1), axis=1)
    position = targets * capacity + arrival
    outgoing = jnp.zeros((encoders * capacity, features), jnp.bfloat16).at[position].set(grad_rows)
    arrived = lax.all_to_all(outgoing, "edata", split_axis=0, concat_axis=0, tiled=True)
    grad_slots = lax.all_gather(arrived, "llm", axis=0, tiled=True)
    stored = stored_context.astype(jnp.float32).reshape(slot_count, -1, BLOCK)
    context = (stored * block_scale[:, :, None]).reshape(slot_count, -1).astype(jnp.bfloat16)
    scaled = (grad_slots.astype(jnp.float32) * layer_scale[None, :]).astype(jnp.bfloat16)
    recomputed = jnp.dot(context, weights, preferred_element_type=jnp.float32)
    grad_context = lax.dot_general(
        scaled, weights, (((1,), (1,)), ((), ())), preferred_element_type=jnp.float32
    ).astype(jnp.bfloat16)
    partial_scale = jnp.sum(grad_slots.astype(jnp.float32) * recomputed, axis=0)
    rescale = 1.0 / math.sqrt(source_rows * encoders * owners)
    grad_weight = (
        lax.psum_scatter(
            lax.dot_general(
                scaled, context, (((0,), (0,)), ((), ())), preferred_element_type=jnp.float32
            ),
            "edata",
            scatter_dimension=0,
            tiled=True,
        )
        * rescale
    )
    grad_scale = lax.psum(partial_scale, ("edata", "llm")) * rescale
    return (grad_context, grad_weight, grad_scale)


def solution(mesh):
    in_specs = (
        P(("edata", "llm"), None),
        P(("edata", "llm"), None),
        P("edata", "llm"),
        P("edata", "llm"),
        P("llm", "edata"),
        P(),
    )
    out_specs = (P("edata", "llm"), P("edata", "llm"), P())
    two_levels = mesh.shape["edata"] == GROUP * GROUP and mesh.shape["llm"] == 2
    return jax.shard_map(
        two_level if two_levels else on_device, mesh=mesh, in_specs=in_specs, out_specs=out_specs, check_vma=False
    )
```

```python
import functools
import math

import jax
import jax.numpy as jnp
from jax import lax
from jax.experimental import pallas as pl
from jax.experimental.pallas import tpu as pltpu
from jax.sharding import PartitionSpec as P

BLOCK = 128
GROUP = 4
MESH = pl.DeviceIdType.MESH


def up(value, unit):
    return -(-value // unit) * unit


def kernel(
    capacity, rescale, gradient_ref, target_ref, stored_ref, block_ref, weight_in_ref, layer_in_ref,
    grad_context_ref, grad_weight_ref, scale_ref,
    gradient, scaled, stored, targets, blocks, weight_own, layer, row_buf, place_buf, routed, arrived, grads, grads_t, contexts,
    weights, context_own, up_out, up_in, down_out, down_in, weight_full, weight_out, weight_in,
    scale_plane, scale_group, scale_all,
    load_sem, row_send, row_recv, place_send, place_recv, weight_send, weight_recv,
    routed_send, routed_recv, cu_send, cu_recv, cd_send, cd_recv, gu_send, gu_recv,
    gd_send, gd_recv, gw_send, gw_recv, plane_send, plane_recv, all_send, all_recv,
):
    e, core = lax.axis_index("edata"), lax.axis_index("llm")
    depth, plane = e // GROUP, e % GROUP
    other = 1 - core
    last = GROUP - 1
    share = weight_own.shape[0]
    features = weights.shape[1]
    slots = stored.shape[0]
    block = routed.shape[1]
    source_rows, width = row_buf.shape[1:]

    def ahead(own, k):
        return (own + k) % GROUP

    def along_depth(k):
        return (ahead(depth, k) * GROUP + plane, core)

    def along_plane(k, owner):
        return (depth * GROUP + ahead(plane, k), owner)

    def send(src, dst, send_sem, recv_sem, device):
        return pltpu.make_async_remote_copy(
            src_ref=src, dst_ref=dst, send_sem=send_sem, recv_sem=recv_sem,
            device_id=device, device_id_type=MESH,
        )

    loads = [
        pltpu.make_async_copy(gradient_ref, gradient, load_sem.at[0]),
        pltpu.make_async_copy(layer_in_ref, layer, load_sem.at[1]),
        pltpu.make_async_copy(target_ref, targets, load_sem.at[2]),
        pltpu.make_async_copy(weight_in_ref, weight_own, load_sem.at[3]),
        pltpu.make_async_copy(stored_ref, stored, load_sem.at[4]),
        pltpu.make_async_copy(block_ref, blocks, load_sem.at[5]),
    ]
    for copy in loads:
        copy.start()
    barrier = pltpu.get_barrier_semaphore()
    for k in range(1, GROUP):
        pl.semaphore_signal(barrier, inc=1, device_id=along_depth(k), device_id_type=MESH)
        for owner in (core, other):
            pl.semaphore_signal(
                barrier, inc=1, device_id=along_plane(k, owner), device_id_type=MESH
            )
    pl.semaphore_signal(barrier, inc=1, device_id=(e, other), device_id_type=MESH)

    loads[2].wait()
    target = jnp.broadcast_to(targets[...], (source_rows, source_rows))
    first = lax.broadcasted_iota(jnp.int32, (source_rows, source_rows), 0)
    second = lax.broadcasted_iota(jnp.int32, (source_rows, source_rows), 1)
    column = target.astype(jnp.float32).T.astype(jnp.int32)
    before = jnp.where((target == column) & (first < second), 1.0, 0.0)
    arrival = jnp.sum(before, axis=0, keepdims=True).astype(jnp.int32)
    target = targets[...]
    place = (target & 3) * block + ((target >> 2) * GROUP + depth) * capacity + arrival
    spread = jnp.concatenate([place] * GROUP, axis=1)
    lane = lax.broadcasted_iota(jnp.int32, spread.shape, 1)
    begin = depth * source_rows
    inside = (lane >= begin) & (lane < begin + source_rows)
    place_buf[depth] = jnp.broadcast_to(jnp.where(inside, spread, 0), place_buf.shape[1:])
    loads[3].wait()
    weights[plane, :share, :] = weight_own[...]
    weights[plane, share:, :] = jnp.zeros((features - share, weights.shape[2]), weights.dtype)
    loads[0].wait()
    loads[1].wait()
    scaled[...] = (gradient[...].astype(jnp.float32) * layer[...].reshape(1, -1)).astype(jnp.bfloat16)
    pl.semaphore_wait(barrier, 3 * last + 1)

    def window(at):
        return pl.multiple_of((at * (GROUP * share)) // BLOCK * BLOCK, BLOCK)

    row_copies = []
    place_copies = []
    for k in range(1, GROUP):
        row_copies.append(
            send(scaled.at[:, pl.ds(window(ahead(depth, k)), width)], row_buf.at[depth],
                 row_send.at[k - 1], row_recv.at[k - 1], along_depth(k))
        )
        place_copies.append(
            send(place_buf.at[depth], place_buf.at[depth],
                 place_send.at[k - 1], place_recv.at[k - 1], along_depth(k))
        )
    for copy in place_copies + row_copies:
        copy.start()
    half = weights.shape[2] // 2
    beside = plane // 2 * 2 + (1 - plane % 2)
    corner = last - plane
    across = (1 - plane // 2) * 2 + plane % 2

    def weight_copy(index, owner, part, to):
        ref = weights.at[owner, :, pl.ds(part * half, half)]
        return send(ref, ref, weight_send.at[index], weight_recv.at[index],
                    (depth * GROUP + to, core))

    weight_copies = [
        weight_copy(0, plane, 0, beside),
        weight_copy(1, plane, 1, across),
        weight_copy(2, plane, 1, beside),
        weight_copy(3, plane, 0, across),
    ]
    for copy in weight_copies:
        copy.start()
    row_buf[depth] = scaled[:, pl.ds(window(depth), width)]

    loads[4].wait()
    loads[5].wait()
    factors = blocks[...].T
    for j in range(factors.shape[1]):
        part = slice(j * BLOCK, (j + 1) * BLOCK)
        contexts[depth, :, part] = (
            stored[:, part].astype(jnp.float32) * factors[:, j : j + 1]
        ).astype(jnp.bfloat16)

    def context_up(s):
        return send(contexts.at[depth - s], contexts.at[depth - s], cu_send.at[s],
                    cu_recv.at[s], ((depth + 1) * GROUP + plane, core))

    def context_down(s):
        return send(contexts.at[depth + s], contexts.at[depth + s], cd_send.at[s],
                    cd_recv.at[s], ((depth - 1) * GROUP + plane, core))

    def context_wait(s):
        @pl.when(depth - 1 - s >= 0)
        def _():
            below = contexts.at[depth - 1 - s]
            send(below, below, cu_send.at[s], cu_recv.at[s], (e, other)).wait_recv()

        @pl.when(depth + 1 + s <= last)
        def _():
            above = contexts.at[depth + 1 + s]
            send(above, above, cd_send.at[s], cd_recv.at[s], (e, other)).wait_recv()

    def context_step(s):
        if s > 0:
            context_wait(s - 1)

        @pl.when((depth < last) & (depth - s >= 0))
        def _():
            context_up(s).start()

        @pl.when((depth > 0) & (depth + s <= last))
        def _():
            context_down(s).start()

    lane = lax.broadcasted_iota(jnp.int32, (1, GROUP * features), 1)
    part = jnp.zeros_like(lane)
    for k in range(1, GROUP):
        part = part + jnp.where(lane >= k * features, 1, 0)
    within = lane - part * features
    source = depth * (GROUP * share) - window(depth) + part * share + within
    source = jnp.where(within < share, source, -1)
    select = jnp.where(
        lax.broadcasted_iota(jnp.int32, (width, GROUP * features), 0) == source, 1.0, 0.0
    ).astype(jnp.bfloat16)

    total = GROUP * slots
    slot = lax.broadcasted_iota(jnp.int32, (total, 1), 0)
    fifth = (slot * (2**18 // capacity + 1)) >> 18
    found_arrival = slot - fifth * capacity
    plane_of, source_depth = fifth & 3, (fifth >> 2) & 3
    core_of, target_depth = (fifth >> 4) & 1, fifth >> 5
    found = (
        (core_of * GROUP + plane_of) * block
        + (target_depth * GROUP + source_depth) * capacity
        + found_arrival
    )
    order = jnp.where(
        lax.broadcasted_iota(jnp.int32, (total, total), 1) == found, 1.0, 0.0
    ).astype(jnp.bfloat16)
    for copy in place_copies:
        copy.wait()
    places = place_buf[0, 0:1, :]
    for j in range(1, GROUP):
        places = places + place_buf[j, 0:1, :]
    wanted = lax.broadcasted_iota(jnp.int32, (GROUP * block, GROUP * source_rows), 0)
    choice = jnp.where(wanted == places, 1.0, 0.0).astype(jnp.bfloat16)
    for copy in row_copies:
        copy.wait()
    context_step(0)
    owned = jnp.dot(
        row_buf[...].reshape(GROUP * source_rows, width), select,
        preferred_element_type=jnp.float32,
    ).astype(jnp.bfloat16)
    routed[...] = (
        jnp.dot(choice, owned, preferred_element_type=jnp.float32)
        .astype(jnp.bfloat16)
        .reshape(GROUP, block, GROUP * features)
    )
    mine = core * GROUP + plane
    routed_copies = [
        send(routed.at[ahead(plane, k)], arrived.at[mine], routed_send.at[k - 1],
             routed_recv.at[k - 1], along_plane(k, core))
        for k in range(1, GROUP)
    ]
    shared_copies = [
        send(routed.at[plane], arrived.at[mine], routed_send.at[last], routed_recv.at[last],
             (e, other))
    ]
    for copy in routed_copies + shared_copies:
        copy.start()
    arrived[mine] = routed[plane]
    weight_copies[0].wait_recv()
    weight_copies[1].wait_recv()
    passed = [weight_copy(4, beside, 0, across), weight_copy(5, across, 1, beside)]
    for copy in passed:
        copy.start()
    for k in range(1, GROUP):
        routed_copies[k - 1].wait_recv()
        block_at = arrived.at[core * GROUP + ahead(plane, GROUP - k)]
        shared_copies.append(
            send(block_at, block_at, routed_send.at[last + k], routed_recv.at[last + k], (e, other))
        )
        shared_copies[-1].start()
    context_step(1)
    for copy in shared_copies:
        copy.wait()
    for copy in routed_copies:
        copy.wait_send()
    ordered = jnp.dot(
        order, arrived[...].reshape(total, GROUP * features), preferred_element_type=jnp.float32
    )
    grads[...] = ordered.astype(jnp.bfloat16).reshape(GROUP, slots, GROUP * features)

    for copy in weight_copies[2:] + passed:
        copy.wait()
    for copy in weight_copies[:2]:
        copy.wait_send()
    upper = depth // (GROUP // 2)

    def own_step(k, carry):
        at = upper * k + (1 - upper) * (last - k)
        context_own[at] = jnp.dot(
            grads[at], weights[...].reshape(GROUP * features, -1),
            preferred_element_type=jnp.float32,
        )
        return carry


    part_rows = slots // 2

    def sum_up(s, h):
        return send(up_out.at[s, h], up_in.at[s, h], gu_send.at[2 * s + h], gu_recv.at[2 * s + h],
                    ((depth + 1) * GROUP + plane, core))

    def sum_down(s, h):
        return send(down_out.at[s, h], down_in.at[s, h], gd_send.at[2 * s + h],
                    gd_recv.at[2 * s + h], ((depth - 1) * GROUP + plane, core))

    def up_wait(s, h):
        ref = up_in.at[s, h]
        send(ref, ref, gu_send.at[2 * s + h], gu_recv.at[2 * s + h], (e, other)).wait_recv()

    def down_wait(s, h):
        ref = down_in.at[s, h]
        send(ref, ref, gd_send.at[2 * s + h], gd_recv.at[2 * s + h], (e, other)).wait_recv()

    def sum_step(s, h):
        piece = slice(h * part_rows, (h + 1) * part_rows)

        @pl.when((depth < last) & (depth <= s))
        def _():
            at = last + depth - s
            if s == 0:
                up_out[s, h] = context_own[at, piece].astype(jnp.bfloat16)
            else:

                @pl.when(depth == 0)
                def _():
                    up_out[s, h] = context_own[at, piece].astype(jnp.bfloat16)

                @pl.when(depth > 0)
                def _():
                    up_wait(s - 1, h)
                    up_out[s, h] = (
                        context_own[at, piece] + up_in[s - 1, h].astype(jnp.float32)
                    ).astype(jnp.bfloat16)

            sum_up(s, h).start()

        @pl.when((depth > 0) & (last - depth <= s))
        def _():
            at = depth - last + s
            if s == 0:
                down_out[s, h] = context_own[at, piece].astype(jnp.bfloat16)
            else:

                @pl.when(depth == last)
                def _():
                    down_out[s, h] = context_own[at, piece].astype(jnp.bfloat16)

                @pl.when(depth < last)
                def _():
                    down_wait(s - 1, h)
                    down_out[s, h] = (
                        context_own[at, piece] + down_in[s - 1, h].astype(jnp.float32)
                    ).astype(jnp.bfloat16)

            sum_down(s, h).start()

    own_step(0, 0)
    sum_step(0, 0)
    sum_step(0, 1)
    lax.fori_loop(1, GROUP, own_step, 0)
    context_step(2)
    grads_t[...] = ordered.T.astype(jnp.bfloat16).reshape(GROUP, features, total)
    sum_step(1, 0)
    sum_step(1, 1)

    context_wait(2)

    def weight_step(at):
        weight_full[at] = jnp.dot(
            grads_t[at], contexts[...].reshape(total, -1), preferred_element_type=jnp.float32
        )

    def columns_of(at, h):
        return weight_full[at, :, h * half : (h + 1) * half]

    def gw_copy(index, to):
        return send(weight_out.at[index], weight_in.at[index], gw_send.at[index],
                    gw_recv.at[index], (depth * GROUP + to, core))

    gw_copies = [gw_copy(i, to) for i, to in enumerate((beside, across) * 2)]
    gw_copies += [gw_copy(4, across), gw_copy(5, beside)]

    def gw_start(index, value):
        weight_out[index] = value.astype(jnp.bfloat16)
        gw_copies[index].start()

    weight_step(corner)
    gw_start(0, columns_of(corner, 0))
    gw_start(1, columns_of(corner, 1))
    weight_step(beside)
    gw_start(2, columns_of(beside, 0))
    weight_step(across)
    gw_start(3, columns_of(across, 1))
    weight_step(plane)
    gw_copies[0].wait_recv()
    gw_start(4, columns_of(across, 0) + weight_in[0].astype(jnp.float32))
    gw_copies[1].wait_recv()
    gw_start(5, columns_of(beside, 1) + weight_in[1].astype(jnp.float32))
    sum_step(2, 0)
    sum_step(2, 1)
    for index in (2, 3, 4, 5):
        gw_copies[index].wait_recv()
    for copy in gw_copies:
        copy.wait_send()
    summed = jnp.concatenate(
        [
            columns_of(plane, h)
            + weight_in[2 + h].astype(jnp.float32)
            + weight_in[4 + h].astype(jnp.float32)
            for h in range(2)
        ],
        axis=1,
    )
    product = summed * weights[plane].astype(jnp.float32)
    lanes = product[:, :BLOCK]
    for j in range(1, product.shape[1] // BLOCK):
        lanes = lanes + product[:, j * BLOCK : (j + 1) * BLOCK]
    own = jnp.sum(lanes.T, axis=0, keepdims=True) * rescale
    pad = scale_plane.shape[2] - features
    own = jnp.broadcast_to(jnp.pad(own, ((0, 0), (0, pad))), scale_plane.shape[1:])

    scale_plane[mine] = own
    plane_copies = []
    for k in range(GROUP):
        for which, owner in enumerate((other, core)):
            if k > 0 or which == 0:
                index = 2 * k + which - (1 if k > 0 else 0)
                plane_copies.append(
                    send(scale_plane.at[mine], scale_plane.at[mine], plane_send.at[index],
                         plane_recv.at[index], along_plane(k, owner))
                )
    for copy in plane_copies:
        copy.start()
    grad_weight_ref[...] = summed[:share, :] * rescale
    for copy in plane_copies:
        copy.wait()
    for j in range(GROUP):
        scale_group[j] = scale_plane[j] + scale_plane[GROUP + j]
    all_copies = [
        send(scale_group, scale_all.at[depth], all_send.at[k - 1], all_recv.at[k - 1],
             along_depth(k))
        for k in range(1, GROUP)
    ]
    for copy in all_copies:
        copy.start()
    scale_all[depth] = scale_group[...]

    for h in range(2):
        piece = slice(h * part_rows, (h + 1) * part_rows)

        @pl.when(depth > 0)
        def _():
            up_wait(last - 1, h)
            context_own[depth, piece] += up_in[last - 1, h].astype(jnp.float32)

        @pl.when(depth < last)
        def _():
            down_wait(last - 1, h)
            context_own[depth, piece] += down_in[last - 1, h].astype(jnp.float32)

        grad_context_ref[piece, :] = context_own[depth, piece].astype(jnp.bfloat16)

    for s in range(last):

        @pl.when((depth < last) & (depth - s >= 0))
        def _():
            context_up(s).wait_send()

        @pl.when((depth > 0) & (depth + s <= last))
        def _():
            context_down(s).wait_send()

        @pl.when((depth < last) & (depth <= s))
        def _():
            for h in range(2):
                sum_up(s, h).wait_send()

        @pl.when((depth > 0) & (last - depth <= s))
        def _():
            for h in range(2):
                sum_down(s, h).wait_send()

    for copy in all_copies:
        copy.wait()
    whole = jnp.concatenate(
        [scale_all[d, q, 0:1, :share] for d in range(GROUP) for q in range(GROUP)], axis=1
    )
    scale_ref[...] = (whole / layer[...].reshape(1, -1)).reshape(-1)


def two_level(grad_rows, row_target, stored_context, block_scale, w_out, layer_scale):
    encoders = lax.axis_size("edata")
    owners = lax.axis_size("llm")
    source_rows, features = grad_rows.shape
    slot_count, columns = stored_context.shape
    capacity = slot_count // (encoders * owners)
    share = features // encoders
    padded = up(share, 16)
    starts = [d * GROUP * share // BLOCK * BLOCK for d in range(GROUP)]
    width = max(up((d + 1) * GROUP * share, BLOCK) - starts[d] for d in range(GROUP))
    block = GROUP * GROUP * capacity
    rescale = 1.0 / math.sqrt(source_rows * encoders * owners)

    total = GROUP * slot_count
    bf16, f32 = jnp.bfloat16, jnp.float32
    small = up(padded, 128)
    sems = [6, 3, 3, 3, 3, 6, 6, 7, 7, 3, 3, 3, 3, 6, 6, 6, 6, 6, 6, 7, 7, 3, 3]
    vmem = pl.BlockSpec(memory_space=pltpu.VMEM)
    far = pl.BlockSpec(memory_space=pltpu.HBM)
    return pl.pallas_call(
        functools.partial(kernel, capacity, rescale),
        out_shape=(
            jax.ShapeDtypeStruct((slot_count, columns), bf16),
            jax.ShapeDtypeStruct((share, columns), f32),
            jax.ShapeDtypeStruct((features,), f32),
        ),
        in_specs=[far] * 6,
        out_specs=[vmem] * 3,
        scratch_shapes=[
            pltpu.VMEM((source_rows, features), bf16),
            pltpu.VMEM((source_rows, features), bf16),
            pltpu.VMEM((slot_count, columns), bf16),
            pltpu.VMEM((1, source_rows), jnp.int32),
            pltpu.VMEM((columns // BLOCK, slot_count), f32),
            pltpu.VMEM((share, columns), bf16),
            pltpu.VMEM((features,), f32),
            pltpu.VMEM((GROUP, source_rows, width), bf16),
            pltpu.VMEM((GROUP, 8, GROUP * source_rows), jnp.int32),
            pltpu.VMEM((GROUP, block, GROUP * padded), bf16),
            pltpu.VMEM((owners * GROUP, block, GROUP * padded), bf16),
            pltpu.VMEM((GROUP, slot_count, GROUP * padded), bf16),
            pltpu.VMEM((GROUP, padded, total), bf16),
            pltpu.VMEM((GROUP, slot_count, columns), bf16),
            pltpu.VMEM((GROUP, padded, columns), bf16),
            pltpu.VMEM((GROUP, slot_count, columns), f32),
            pltpu.VMEM((GROUP - 1, 2, slot_count // 2, columns), bf16),
            pltpu.VMEM((GROUP - 1, 2, slot_count // 2, columns), bf16),
            pltpu.VMEM((GROUP - 1, 2, slot_count // 2, columns), bf16),
            pltpu.VMEM((GROUP - 1, 2, slot_count // 2, columns), bf16),
            pltpu.VMEM((GROUP, padded, columns), f32),
            pltpu.VMEM((6, padded, columns // 2), bf16),
            pltpu.VMEM((6, padded, columns // 2), bf16),
            pltpu.VMEM((owners * GROUP, 8, small), f32),
            pltpu.VMEM((GROUP, 8, small), f32),
            pltpu.VMEM((GROUP, GROUP, 8, small), f32),
        ]
        + [pltpu.SemaphoreType.DMA((n,)) for n in sems],
        compiler_params=pltpu.CompilerParams(
            collective_id=0, has_side_effects=True, vmem_limit_bytes=64 * 2**20
        ),
    )(grad_rows, row_target.T, stored_context, block_scale.T, w_out.T, layer_scale)


def on_device(grad_rows, row_target, stored_context, block_scale, w_out, layer_scale):
    encoders = lax.axis_size("edata")
    owners = lax.axis_size("llm")
    source_rows = grad_rows.shape[0]
    features = grad_rows.shape[1]
    slot_count = stored_context.shape[0]
    capacity = slot_count // (encoders * owners)
    weights = lax.all_gather(w_out, "edata", axis=1, tiled=True)
    targets = row_target[:, 0]
    chosen = (targets[:, None] == jnp.arange(encoders, dtype=jnp.int32)[None, :]).astype(jnp.int32)
    arrival = jnp.sum(chosen * (jnp.cumsum(chosen, axis=0) - 1), axis=1)
    position = targets * capacity + arrival
    outgoing = jnp.zeros((encoders * capacity, features), jnp.bfloat16).at[position].set(grad_rows)
    arrived = lax.all_to_all(outgoing, "edata", split_axis=0, concat_axis=0, tiled=True)
    grad_slots = lax.all_gather(arrived, "llm", axis=0, tiled=True)
    stored = stored_context.astype(jnp.float32).reshape(slot_count, -1, BLOCK)
    context = (stored * block_scale[:, :, None]).reshape(slot_count, -1).astype(jnp.bfloat16)
    scaled = (grad_slots.astype(jnp.float32) * layer_scale[None, :]).astype(jnp.bfloat16)
    recomputed = jnp.dot(context, weights, preferred_element_type=jnp.float32)
    grad_context = lax.dot_general(
        scaled, weights, (((1,), (1,)), ((), ())), preferred_element_type=jnp.float32
    ).astype(jnp.bfloat16)
    partial_scale = jnp.sum(grad_slots.astype(jnp.float32) * recomputed, axis=0)
    rescale = 1.0 / math.sqrt(source_rows * encoders * owners)
    grad_weight = (
        lax.psum_scatter(
            lax.dot_general(
                scaled, context, (((0,), (0,)), ((), ())), preferred_element_type=jnp.float32
            ),
            "edata",
            scatter_dimension=0,
            tiled=True,
        )
        * rescale
    )
    grad_scale = lax.psum(partial_scale, ("edata", "llm")) * rescale
    return (grad_context, grad_weight, grad_scale)


def solution(mesh):
    in_specs = (
        P(("edata", "llm"), None),
        P(("edata", "llm"), None),
        P("edata", "llm"),
        P("edata", "llm"),
        P("llm", "edata"),
        P(),
    )
    out_specs = (P("edata", "llm"), P("edata", "llm"), P())
    two_levels = mesh.shape["edata"] == GROUP * GROUP and mesh.shape["llm"] == 2
    return jax.shard_map(
        two_level if two_levels else on_device, mesh=mesh, in_specs=in_specs, out_specs=out_specs, check_vma=False
    )
```

```python
import functools
import math

import jax
import jax.numpy as jnp
from jax import lax
from jax.experimental import pallas as pl
from jax.experimental.pallas import tpu as pltpu
from jax.sharding import PartitionSpec as P

BLOCK = 128
GROUP = 4
MESH = pl.DeviceIdType.MESH


def up(value, unit):
    return -(-value // unit) * unit


def kernel(
    capacity, rescale, gradient_ref, target_ref, stored_ref, block_ref, weight_in_ref, layer_in_ref,
    grad_context_ref, grad_weight_ref, scale_ref,
    gradient, scaled, stored, targets, blocks, weight_own, layer, row_buf, place_buf, routed, arrived, grads, grads_t, contexts,
    weights, context_own, up_out, up_in, down_out, down_in, weight_full, weight_out, weight_in,
    scale_plane, scale_group, scale_all,
    load_sem, row_send, row_recv, place_send, place_recv, weight_send, weight_recv,
    routed_send, routed_recv, cu_send, cu_recv, cd_send, cd_recv, gu_send, gu_recv,
    gd_send, gd_recv, gw_send, gw_recv, plane_send, plane_recv, all_send, all_recv,
):
    e, core = lax.axis_index("edata"), lax.axis_index("llm")
    depth, plane = e // GROUP, e % GROUP
    other = 1 - core
    last = GROUP - 1
    share = weight_own.shape[0]
    features = weights.shape[1]
    slots = stored.shape[0]
    block = routed.shape[1]
    source_rows, width = row_buf.shape[1:]

    def ahead(own, k):
        return (own + k) % GROUP

    def along_depth(k):
        return (ahead(depth, k) * GROUP + plane, core)

    def along_plane(k, owner):
        return (depth * GROUP + ahead(plane, k), owner)

    def send(src, dst, send_sem, recv_sem, device):
        return pltpu.make_async_remote_copy(
            src_ref=src, dst_ref=dst, send_sem=send_sem, recv_sem=recv_sem,
            device_id=device, device_id_type=MESH,
        )

    loads = [
        pltpu.make_async_copy(gradient_ref, gradient, load_sem.at[0]),
        pltpu.make_async_copy(layer_in_ref, layer, load_sem.at[1]),
        pltpu.make_async_copy(target_ref, targets, load_sem.at[2]),
        pltpu.make_async_copy(weight_in_ref, weight_own, load_sem.at[3]),
        pltpu.make_async_copy(stored_ref, stored, load_sem.at[4]),
        pltpu.make_async_copy(block_ref, blocks, load_sem.at[5]),
    ]
    for copy in loads:
        copy.start()
    barrier = pltpu.get_barrier_semaphore()
    for k in range(1, GROUP):
        pl.semaphore_signal(barrier, inc=1, device_id=along_depth(k), device_id_type=MESH)
        for owner in (core, other):
            pl.semaphore_signal(
                barrier, inc=1, device_id=along_plane(k, owner), device_id_type=MESH
            )
    pl.semaphore_signal(barrier, inc=1, device_id=(e, other), device_id_type=MESH)

    loads[2].wait()
    target = jnp.broadcast_to(targets[...], (source_rows, source_rows))
    first = lax.broadcasted_iota(jnp.int32, (source_rows, source_rows), 0)
    second = lax.broadcasted_iota(jnp.int32, (source_rows, source_rows), 1)
    column = target.astype(jnp.float32).T.astype(jnp.int32)
    before = jnp.where((target == column) & (first < second), 1.0, 0.0)
    arrival = jnp.sum(before, axis=0, keepdims=True).astype(jnp.int32)
    target = targets[...]
    place = (target & 3) * block + ((target >> 2) * GROUP + depth) * capacity + arrival
    spread = jnp.concatenate([place] * GROUP, axis=1)
    lane = lax.broadcasted_iota(jnp.int32, spread.shape, 1)
    begin = depth * source_rows
    inside = (lane >= begin) & (lane < begin + source_rows)
    place_buf[depth] = jnp.broadcast_to(jnp.where(inside, spread, 0), place_buf.shape[1:])
    loads[3].wait()
    weights[plane, :share, :] = weight_own[...]
    weights[plane, share:, :] = jnp.zeros((features - share, weights.shape[2]), weights.dtype)
    loads[0].wait()
    loads[1].wait()
    scaled[...] = (gradient[...].astype(jnp.float32) * layer[...].reshape(1, -1)).astype(jnp.bfloat16)
    pl.semaphore_wait(barrier, 3 * last + 1)

    def window(at):
        return pl.multiple_of((at * (GROUP * share)) // BLOCK * BLOCK, BLOCK)

    row_copies = []
    place_copies = []
    for k in range(1, GROUP):
        row_copies.append(
            send(scaled.at[:, pl.ds(window(ahead(depth, k)), width)], row_buf.at[depth],
                 row_send.at[k - 1], row_recv.at[k - 1], along_depth(k))
        )
        place_copies.append(
            send(place_buf.at[depth], place_buf.at[depth],
                 place_send.at[k - 1], place_recv.at[k - 1], along_depth(k))
        )
    for copy in place_copies + row_copies:
        copy.start()
    half = weights.shape[2] // 2
    beside = plane // 2 * 2 + (1 - plane % 2)
    corner = last - plane
    across = (1 - plane // 2) * 2 + plane % 2

    def weight_copy(index, owner, part, to):
        ref = weights.at[owner, :, pl.ds(part * half, half)]
        return send(ref, ref, weight_send.at[index], weight_recv.at[index],
                    (depth * GROUP + to, core))

    weight_copies = [
        weight_copy(0, plane, 0, beside),
        weight_copy(1, plane, 1, across),
        weight_copy(2, plane, 1, beside),
        weight_copy(3, plane, 0, across),
    ]
    for copy in weight_copies:
        copy.start()
    row_buf[depth] = scaled[:, pl.ds(window(depth), width)]

    loads[4].wait()
    loads[5].wait()
    factors = blocks[...].T
    for j in range(factors.shape[1]):
        part = slice(j * BLOCK, (j + 1) * BLOCK)
        contexts[depth, :, part] = (
            stored[:, part].astype(jnp.float32) * factors[:, j : j + 1]
        ).astype(jnp.bfloat16)

    def context_up(s):
        return send(contexts.at[depth - s], contexts.at[depth - s], cu_send.at[s],
                    cu_recv.at[s], ((depth + 1) * GROUP + plane, core))

    def context_down(s):
        return send(contexts.at[depth + s], contexts.at[depth + s], cd_send.at[s],
                    cd_recv.at[s], ((depth - 1) * GROUP + plane, core))

    def context_wait(s):
        @pl.when(depth - 1 - s >= 0)
        def _():
            below = contexts.at[depth - 1 - s]
            send(below, below, cu_send.at[s], cu_recv.at[s], (e, other)).wait_recv()

        @pl.when(depth + 1 + s <= last)
        def _():
            above = contexts.at[depth + 1 + s]
            send(above, above, cd_send.at[s], cd_recv.at[s], (e, other)).wait_recv()

    def context_step(s):
        if s > 0:
            context_wait(s - 1)

        @pl.when((depth < last) & (depth - s >= 0))
        def _():
            context_up(s).start()

        @pl.when((depth > 0) & (depth + s <= last))
        def _():
            context_down(s).start()

    context_step(0)

    lane = lax.broadcasted_iota(jnp.int32, (1, GROUP * features), 1)
    part = jnp.zeros_like(lane)
    for k in range(1, GROUP):
        part = part + jnp.where(lane >= k * features, 1, 0)
    within = lane - part * features
    source = depth * (GROUP * share) - window(depth) + part * share + within
    source = jnp.where(within < share, source, -1)
    select = jnp.where(
        lax.broadcasted_iota(jnp.int32, (width, GROUP * features), 0) == source, 1.0, 0.0
    ).astype(jnp.bfloat16)

    total = GROUP * slots
    slot = lax.broadcasted_iota(jnp.int32, (total, 1), 0)
    fifth = (slot * (2**18 // capacity + 1)) >> 18
    found_arrival = slot - fifth * capacity
    plane_of, source_depth = fifth & 3, (fifth >> 2) & 3
    core_of, target_depth = (fifth >> 4) & 1, fifth >> 5
    found = (
        (core_of * GROUP + plane_of) * block
        + (target_depth * GROUP + source_depth) * capacity
        + found_arrival
    )
    order = jnp.where(
        lax.broadcasted_iota(jnp.int32, (total, total), 1) == found, 1.0, 0.0
    ).astype(jnp.bfloat16)
    weight_copies[0].wait_recv()
    weight_copies[1].wait_recv()
    passed = [weight_copy(4, beside, 0, across), weight_copy(5, across, 1, beside)]
    for copy in passed:
        copy.start()

    for copy in place_copies:
        copy.wait()
    places = place_buf[0, 0:1, :]
    for j in range(1, GROUP):
        places = places + place_buf[j, 0:1, :]
    wanted = lax.broadcasted_iota(jnp.int32, (GROUP * block, GROUP * source_rows), 0)
    choice = jnp.where(wanted == places, 1.0, 0.0).astype(jnp.bfloat16)
    for copy in row_copies:
        copy.wait()
    owned = jnp.dot(
        row_buf[...].reshape(GROUP * source_rows, width), select,
        preferred_element_type=jnp.float32,
    ).astype(jnp.bfloat16)
    routed[...] = (
        jnp.dot(choice, owned, preferred_element_type=jnp.float32)
        .astype(jnp.bfloat16)
        .reshape(GROUP, block, GROUP * features)
    )
    mine = core * GROUP + plane
    routed_copies = [
        send(routed.at[ahead(plane, k)], arrived.at[mine], routed_send.at[k - 1],
             routed_recv.at[k - 1], along_plane(k, core))
        for k in range(1, GROUP)
    ]
    shared_copies = [
        send(routed.at[plane], arrived.at[mine], routed_send.at[last], routed_recv.at[last],
             (e, other))
    ]
    for copy in routed_copies + shared_copies:
        copy.start()
    arrived[mine] = routed[plane]
    context_step(1)
    for k in range(1, GROUP):
        routed_copies[k - 1].wait_recv()
        block_at = arrived.at[core * GROUP + ahead(plane, GROUP - k)]
        shared_copies.append(
            send(block_at, block_at, routed_send.at[last + k], routed_recv.at[last + k], (e, other))
        )
        shared_copies[-1].start()
    for copy in shared_copies:
        copy.wait()
    for copy in routed_copies:
        copy.wait_send()
    ordered = jnp.dot(
        order, arrived[...].reshape(total, GROUP * features), preferred_element_type=jnp.float32
    )
    grads[...] = ordered.astype(jnp.bfloat16).reshape(GROUP, slots, GROUP * features)

    for copy in weight_copies[2:] + passed:
        copy.wait()
    for copy in weight_copies[:2]:
        copy.wait_send()
    upper = depth // (GROUP // 2)

    def own_step(k, carry):
        at = upper * k + (1 - upper) * (last - k)
        context_own[at] = jnp.dot(
            grads[at], weights[...].reshape(GROUP * features, -1),
            preferred_element_type=jnp.float32,
        )
        return carry


    part_rows = slots // 2

    def sum_up(s, h):
        return send(up_out.at[s, h], up_in.at[s, h], gu_send.at[2 * s + h], gu_recv.at[2 * s + h],
                    ((depth + 1) * GROUP + plane, core))

    def sum_down(s, h):
        return send(down_out.at[s, h], down_in.at[s, h], gd_send.at[2 * s + h],
                    gd_recv.at[2 * s + h], ((depth - 1) * GROUP + plane, core))

    def up_wait(s, h):
        ref = up_in.at[s, h]
        send(ref, ref, gu_send.at[2 * s + h], gu_recv.at[2 * s + h], (e, other)).wait_recv()

    def down_wait(s, h):
        ref = down_in.at[s, h]
        send(ref, ref, gd_send.at[2 * s + h], gd_recv.at[2 * s + h], (e, other)).wait_recv()

    def sum_step(s, h):
        piece = slice(h * part_rows, (h + 1) * part_rows)

        @pl.when((depth < last) & (depth <= s))
        def _():
            at = last + depth - s
            if s == 0:
                up_out[s, h] = context_own[at, piece].astype(jnp.bfloat16)
            else:

                @pl.when(depth == 0)
                def _():
                    up_out[s, h] = context_own[at, piece].astype(jnp.bfloat16)

                @pl.when(depth > 0)
                def _():
                    up_wait(s - 1, h)
                    up_out[s, h] = (
                        context_own[at, piece] + up_in[s - 1, h].astype(jnp.float32)
                    ).astype(jnp.bfloat16)

            sum_up(s, h).start()

        @pl.when((depth > 0) & (last - depth <= s))
        def _():
            at = depth - last + s
            if s == 0:
                down_out[s, h] = context_own[at, piece].astype(jnp.bfloat16)
            else:

                @pl.when(depth == last)
                def _():
                    down_out[s, h] = context_own[at, piece].astype(jnp.bfloat16)

                @pl.when(depth < last)
                def _():
                    down_wait(s - 1, h)
                    down_out[s, h] = (
                        context_own[at, piece] + down_in[s - 1, h].astype(jnp.float32)
                    ).astype(jnp.bfloat16)

            sum_down(s, h).start()

    own_step(0, 0)
    sum_step(0, 0)
    sum_step(0, 1)
    context_step(2)
    lax.fori_loop(1, GROUP, own_step, 0)
    grads_t[...] = ordered.T.astype(jnp.bfloat16).reshape(GROUP, features, total)
    sum_step(1, 0)
    sum_step(1, 1)

    context_wait(2)

    def weight_step(at):
        weight_full[at] = jnp.dot(
            grads_t[at], contexts[...].reshape(total, -1), preferred_element_type=jnp.float32
        )

    def columns_of(at, h):
        return weight_full[at, :, h * half : (h + 1) * half]

    def gw_copy(index, to):
        return send(weight_out.at[index], weight_in.at[index], gw_send.at[index],
                    gw_recv.at[index], (depth * GROUP + to, core))

    gw_copies = [gw_copy(i, to) for i, to in enumerate((beside, across) * 2)]
    gw_copies += [gw_copy(4, across), gw_copy(5, beside)]

    def gw_start(index, value):
        weight_out[index] = value.astype(jnp.bfloat16)
        gw_copies[index].start()

    weight_step(corner)
    gw_start(0, columns_of(corner, 0))
    gw_start(1, columns_of(corner, 1))
    weight_step(beside)
    gw_start(2, columns_of(beside, 0))
    weight_step(across)
    gw_start(3, columns_of(across, 1))
    weight_step(plane)
    gw_copies[0].wait_recv()
    gw_start(4, columns_of(across, 0) + weight_in[0].astype(jnp.float32))
    gw_copies[1].wait_recv()
    gw_start(5, columns_of(beside, 1) + weight_in[1].astype(jnp.float32))
    sum_step(2, 0)
    sum_step(2, 1)
    for index in (2, 3, 4, 5):
        gw_copies[index].wait_recv()
    for copy in gw_copies:
        copy.wait_send()
    summed = jnp.concatenate(
        [
            columns_of(plane, h)
            + weight_in[2 + h].astype(jnp.float32)
            + weight_in[4 + h].astype(jnp.float32)
            for h in range(2)
        ],
        axis=1,
    )
    product = summed * weights[plane].astype(jnp.float32)
    lanes = product[:, :BLOCK]
    for j in range(1, product.shape[1] // BLOCK):
        lanes = lanes + product[:, j * BLOCK : (j + 1) * BLOCK]
    own = jnp.sum(lanes.T, axis=0, keepdims=True) * rescale
    pad = scale_plane.shape[2] - features
    own = jnp.broadcast_to(jnp.pad(own, ((0, 0), (0, pad))), scale_plane.shape[1:])

    scale_plane[mine] = own
    plane_copies = []
    for k in range(GROUP):
        for which, owner in enumerate((other, core)):
            if k > 0 or which == 0:
                index = 2 * k + which - (1 if k > 0 else 0)
                plane_copies.append(
                    send(scale_plane.at[mine], scale_plane.at[mine], plane_send.at[index],
                         plane_recv.at[index], along_plane(k, owner))
                )
    for copy in plane_copies:
        copy.start()
    grad_weight_ref[...] = summed[:share, :] * rescale
    for copy in plane_copies:
        copy.wait()
    for j in range(GROUP):
        scale_group[j] = scale_plane[j] + scale_plane[GROUP + j]
    all_copies = [
        send(scale_group, scale_all.at[depth], all_send.at[k - 1], all_recv.at[k - 1],
             along_depth(k))
        for k in range(1, GROUP)
    ]
    for copy in all_copies:
        copy.start()
    scale_all[depth] = scale_group[...]

    for h in range(2):
        piece = slice(h * part_rows, (h + 1) * part_rows)

        @pl.when(depth > 0)
        def _():
            up_wait(last - 1, h)
            context_own[depth, piece] += up_in[last - 1, h].astype(jnp.float32)

        @pl.when(depth < last)
        def _():
            down_wait(last - 1, h)
            context_own[depth, piece] += down_in[last - 1, h].astype(jnp.float32)

        grad_context_ref[piece, :] = context_own[depth, piece].astype(jnp.bfloat16)

    for s in range(last):

        @pl.when((depth < last) & (depth - s >= 0))
        def _():
            context_up(s).wait_send()

        @pl.when((depth > 0) & (depth + s <= last))
        def _():
            context_down(s).wait_send()

        @pl.when((depth < last) & (depth <= s))
        def _():
            for h in range(2):
                sum_up(s, h).wait_send()

        @pl.when((depth > 0) & (last - depth <= s))
        def _():
            for h in range(2):
                sum_down(s, h).wait_send()

    for copy in all_copies:
        copy.wait()
    whole = jnp.concatenate(
        [scale_all[d, q, 0:1, :share] for d in range(GROUP) for q in range(GROUP)], axis=1
    )
    scale_ref[...] = (whole / layer[...].reshape(1, -1)).reshape(-1)


def two_level(grad_rows, row_target, stored_context, block_scale, w_out, layer_scale):
    encoders = lax.axis_size("edata")
    owners = lax.axis_size("llm")
    source_rows, features = grad_rows.shape
    slot_count, columns = stored_context.shape
    capacity = slot_count // (encoders * owners)
    share = features // encoders
    padded = up(share, 16)
    starts = [d * GROUP * share // BLOCK * BLOCK for d in range(GROUP)]
    width = max(up((d + 1) * GROUP * share, BLOCK) - starts[d] for d in range(GROUP))
    block = GROUP * GROUP * capacity
    rescale = 1.0 / math.sqrt(source_rows * encoders * owners)

    total = GROUP * slot_count
    bf16, f32 = jnp.bfloat16, jnp.float32
    small = up(padded, 128)
    sems = [6, 3, 3, 3, 3, 6, 6, 7, 7, 3, 3, 3, 3, 6, 6, 6, 6, 6, 6, 7, 7, 3, 3]
    vmem = pl.BlockSpec(memory_space=pltpu.VMEM)
    far = pl.BlockSpec(memory_space=pltpu.HBM)
    return pl.pallas_call(
        functools.partial(kernel, capacity, rescale),
        out_shape=(
            pltpu.VMEM((slot_count, columns), bf16),
            pltpu.VMEM((share, columns), f32),
            pltpu.VMEM((features,), f32),
        ),
        in_specs=[far] * 6,
        out_specs=[vmem] * 3,
        scratch_shapes=[
            pltpu.VMEM((source_rows, features), bf16),
            pltpu.VMEM((source_rows, features), bf16),
            pltpu.VMEM((slot_count, columns), bf16),
            pltpu.VMEM((1, source_rows), jnp.int32),
            pltpu.VMEM((columns // BLOCK, slot_count), f32),
            pltpu.VMEM((share, columns), bf16),
            pltpu.VMEM((features,), f32),
            pltpu.VMEM((GROUP, source_rows, width), bf16),
            pltpu.VMEM((GROUP, 8, GROUP * source_rows), jnp.int32),
            pltpu.VMEM((GROUP, block, GROUP * padded), bf16),
            pltpu.VMEM((owners * GROUP, block, GROUP * padded), bf16),
            pltpu.VMEM((GROUP, slot_count, GROUP * padded), bf16),
            pltpu.VMEM((GROUP, padded, total), bf16),
            pltpu.VMEM((GROUP, slot_count, columns), bf16),
            pltpu.VMEM((GROUP, padded, columns), bf16),
            pltpu.VMEM((GROUP, slot_count, columns), f32),
            pltpu.VMEM((GROUP - 1, 2, slot_count // 2, columns), bf16),
            pltpu.VMEM((GROUP - 1, 2, slot_count // 2, columns), bf16),
            pltpu.VMEM((GROUP - 1, 2, slot_count // 2, columns), bf16),
            pltpu.VMEM((GROUP - 1, 2, slot_count // 2, columns), bf16),
            pltpu.VMEM((GROUP, padded, columns), f32),
            pltpu.VMEM((6, padded, columns // 2), bf16),
            pltpu.VMEM((6, padded, columns // 2), bf16),
            pltpu.VMEM((owners * GROUP, 8, small), f32),
            pltpu.VMEM((GROUP, 8, small), f32),
            pltpu.VMEM((GROUP, GROUP, 8, small), f32),
        ]
        + [pltpu.SemaphoreType.DMA((n,)) for n in sems],
        compiler_params=pltpu.CompilerParams(
            collective_id=0, has_side_effects=True, vmem_limit_bytes=48 * 2**20
        ),
    )(
        *[
            pltpu.with_memory_space_constraint(array, pltpu.HBM)
            for array in (
                grad_rows, row_target.T, stored_context, block_scale.T, w_out.T, layer_scale
            )
        ]
    )


def on_device(grad_rows, row_target, stored_context, block_scale, w_out, layer_scale):
    encoders = lax.axis_size("edata")
    owners = lax.axis_size("llm")
    source_rows = grad_rows.shape[0]
    features = grad_rows.shape[1]
    slot_count = stored_context.shape[0]
    capacity = slot_count // (encoders * owners)
    weights = lax.all_gather(w_out, "edata", axis=1, tiled=True)
    targets = row_target[:, 0]
    chosen = (targets[:, None] == jnp.arange(encoders, dtype=jnp.int32)[None, :]).astype(jnp.int32)
    arrival = jnp.sum(chosen * (jnp.cumsum(chosen, axis=0) - 1), axis=1)
    position = targets * capacity + arrival
    outgoing = jnp.zeros((encoders * capacity, features), jnp.bfloat16).at[position].set(grad_rows)
    arrived = lax.all_to_all(outgoing, "edata", split_axis=0, concat_axis=0, tiled=True)
    grad_slots = lax.all_gather(arrived, "llm", axis=0, tiled=True)
    stored = stored_context.astype(jnp.float32).reshape(slot_count, -1, BLOCK)
    context = (stored * block_scale[:, :, None]).reshape(slot_count, -1).astype(jnp.bfloat16)
    scaled = (grad_slots.astype(jnp.float32) * layer_scale[None, :]).astype(jnp.bfloat16)
    recomputed = jnp.dot(context, weights, preferred_element_type=jnp.float32)
    grad_context = lax.dot_general(
        scaled, weights, (((1,), (1,)), ((), ())), preferred_element_type=jnp.float32
    ).astype(jnp.bfloat16)
    partial_scale = jnp.sum(grad_slots.astype(jnp.float32) * recomputed, axis=0)
    rescale = 1.0 / math.sqrt(source_rows * encoders * owners)
    grad_weight = (
        lax.psum_scatter(
            lax.dot_general(
                scaled, context, (((0,), (0,)), ((), ())), preferred_element_type=jnp.float32
            ),
            "edata",
            scatter_dimension=0,
            tiled=True,
        )
        * rescale
    )
    grad_scale = lax.psum(partial_scale, ("edata", "llm")) * rescale
    return (grad_context, grad_weight, grad_scale)


def solution(mesh):
    in_specs = (
        P(("edata", "llm"), None),
        P(("edata", "llm"), None),
        P("edata", "llm"),
        P("edata", "llm"),
        P("llm", "edata"),
        P(),
    )
    out_specs = (P("edata", "llm"), P("edata", "llm"), P())
    two_levels = mesh.shape["edata"] == GROUP * GROUP and mesh.shape["llm"] == 2
    return jax.shard_map(
        two_level if two_levels else on_device, mesh=mesh, in_specs=in_specs, out_specs=out_specs, check_vma=False
    )
```

```python
import functools
import math

import jax
import jax.numpy as jnp
from jax import lax
from jax.experimental import pallas as pl
from jax.experimental.pallas import tpu as pltpu
from jax.sharding import PartitionSpec as P

BLOCK = 128
GROUP = 4
MESH = pl.DeviceIdType.MESH


def up(value, unit):
    return -(-value // unit) * unit


def kernel(
    capacity, rescale, gradient_ref, target_ref, stored_ref, block_ref, weight_in_ref, layer_in_ref,
    grad_context_ref, grad_weight_ref, scale_ref,
    gradient, scaled, stored, targets, blocks, weight_own, layer, row_buf, place_buf, routed, arrived, grads, grads_t, contexts,
    weights, context_own, up_out, up_in, down_out, down_in, weight_full, weight_out, weight_in,
    scale_plane, scale_group, scale_all,
    load_sem, row_send, row_recv, place_send, place_recv, weight_send, weight_recv,
    routed_send, routed_recv, cu_send, cu_recv, cd_send, cd_recv, gu_send, gu_recv,
    gd_send, gd_recv, gw_send, gw_recv, plane_send, plane_recv, all_send, all_recv,
):
    e, core = lax.axis_index("edata"), lax.axis_index("llm")
    depth, plane = e // GROUP, e % GROUP
    other = 1 - core
    last = GROUP - 1
    share = weight_own.shape[0]
    features = weights.shape[1]
    slots = stored.shape[0]
    block = routed.shape[1]
    source_rows, width = row_buf.shape[1:]

    def ahead(own, k):
        return (own + k) % GROUP

    def along_depth(k):
        return (ahead(depth, k) * GROUP + plane, core)

    def along_plane(k, owner):
        return (depth * GROUP + ahead(plane, k), owner)

    def send(src, dst, send_sem, recv_sem, device):
        return pltpu.make_async_remote_copy(
            src_ref=src, dst_ref=dst, send_sem=send_sem, recv_sem=recv_sem,
            device_id=device, device_id_type=MESH,
        )

    loads = [
        pltpu.make_async_copy(gradient_ref, gradient, load_sem.at[0]),
        pltpu.make_async_copy(layer_in_ref, layer, load_sem.at[1]),
        pltpu.make_async_copy(target_ref, targets, load_sem.at[2]),
        pltpu.make_async_copy(weight_in_ref, weight_own, load_sem.at[3]),
        pltpu.make_async_copy(stored_ref, stored, load_sem.at[4]),
        pltpu.make_async_copy(block_ref, blocks, load_sem.at[5]),
    ]
    for copy in loads:
        copy.start()
    barrier = pltpu.get_barrier_semaphore()
    for k in range(1, GROUP):
        pl.semaphore_signal(barrier, inc=1, device_id=along_depth(k), device_id_type=MESH)
        for owner in (core, other):
            pl.semaphore_signal(
                barrier, inc=1, device_id=along_plane(k, owner), device_id_type=MESH
            )
    pl.semaphore_signal(barrier, inc=1, device_id=(e, other), device_id_type=MESH)

    loads[2].wait()
    target = jnp.broadcast_to(targets[...], (source_rows, source_rows))
    first = lax.broadcasted_iota(jnp.int32, (source_rows, source_rows), 0)
    second = lax.broadcasted_iota(jnp.int32, (source_rows, source_rows), 1)
    column = target.astype(jnp.float32).T.astype(jnp.int32)
    before = jnp.where((target == column) & (first < second), 1.0, 0.0)
    arrival = jnp.sum(before, axis=0, keepdims=True).astype(jnp.int32)
    target = targets[...]
    place = (target & 3) * block + ((target >> 2) * GROUP + depth) * capacity + arrival
    spread = jnp.concatenate([place] * GROUP, axis=1)
    lane = lax.broadcasted_iota(jnp.int32, spread.shape, 1)
    begin = depth * source_rows
    inside = (lane >= begin) & (lane < begin + source_rows)
    place_buf[depth] = jnp.broadcast_to(jnp.where(inside, spread, 0), place_buf.shape[1:])
    loads[3].wait()
    weights[plane, :share, :] = weight_own[...]
    weights[plane, share:, :] = jnp.zeros((features - share, weights.shape[2]), weights.dtype)
    loads[0].wait()
    loads[1].wait()
    scaled[...] = (gradient[...].astype(jnp.float32) * layer[...].reshape(1, -1)).astype(jnp.bfloat16)
    pl.semaphore_wait(barrier, 3 * last + 1)

    def window(at):
        return pl.multiple_of((at * (GROUP * share)) // BLOCK * BLOCK, BLOCK)

    row_copies = []
    place_copies = []
    for k in range(1, GROUP):
        row_copies.append(
            send(scaled.at[:, pl.ds(window(ahead(depth, k)), width)], row_buf.at[depth],
                 row_send.at[k - 1], row_recv.at[k - 1], along_depth(k))
        )
        place_copies.append(
            send(place_buf.at[depth], place_buf.at[depth],
                 place_send.at[k - 1], place_recv.at[k - 1], along_depth(k))
        )
    for copy in place_copies + row_copies:
        copy.start()
    half = weights.shape[2] // 2
    beside = plane // 2 * 2 + (1 - plane % 2)
    corner = last - plane
    across = (1 - plane // 2) * 2 + plane % 2

    def weight_copy(index, owner, part, to):
        ref = weights.at[owner, :, pl.ds(part * half, half)]
        return send(ref, ref, weight_send.at[index], weight_recv.at[index],
                    (depth * GROUP + to, core))

    weight_copies = [
        weight_copy(0, plane, 0, beside),
        weight_copy(1, plane, 1, across),
        weight_copy(2, plane, 1, beside),
        weight_copy(3, plane, 0, across),
    ]
    for copy in weight_copies:
        copy.start()
    row_buf[depth] = scaled[:, pl.ds(window(depth), width)]

    loads[4].wait()
    loads[5].wait()
    factors = blocks[...].T
    for j in range(factors.shape[1]):
        part = slice(j * BLOCK, (j + 1) * BLOCK)
        contexts[depth, :, part] = (
            stored[:, part].astype(jnp.float32) * factors[:, j : j + 1]
        ).astype(jnp.bfloat16)

    def context_up(s):
        return send(contexts.at[depth - s], contexts.at[depth - s], cu_send.at[s],
                    cu_recv.at[s], ((depth + 1) * GROUP + plane, core))

    def context_down(s):
        return send(contexts.at[depth + s], contexts.at[depth + s], cd_send.at[s],
                    cd_recv.at[s], ((depth - 1) * GROUP + plane, core))

    def context_wait(s):
        @pl.when(depth - 1 - s >= 0)
        def _():
            below = contexts.at[depth - 1 - s]
            send(below, below, cu_send.at[s], cu_recv.at[s], (e, other)).wait_recv()

        @pl.when(depth + 1 + s <= last)
        def _():
            above = contexts.at[depth + 1 + s]
            send(above, above, cd_send.at[s], cd_recv.at[s], (e, other)).wait_recv()

    def context_step(s):
        if s > 0:
            context_wait(s - 1)

        @pl.when((depth < last) & (depth - s >= 0))
        def _():
            context_up(s).start()

        @pl.when((depth > 0) & (depth + s <= last))
        def _():
            context_down(s).start()

    context_step(0)

    lane = lax.broadcasted_iota(jnp.int32, (1, GROUP * features), 1)
    part = jnp.zeros_like(lane)
    for k in range(1, GROUP):
        part = part + jnp.where(lane >= k * features, 1, 0)
    within = lane - part * features
    source = depth * (GROUP * share) - window(depth) + part * share + within
    source = jnp.where(within < share, source, -1)
    select = jnp.where(
        lax.broadcasted_iota(jnp.int32, (width, GROUP * features), 0) == source, 1.0, 0.0
    ).astype(jnp.bfloat16)

    total = GROUP * slots
    slot = lax.broadcasted_iota(jnp.int32, (total, 1), 0)
    fifth = (slot * (2**18 // capacity + 1)) >> 18
    found_arrival = slot - fifth * capacity
    plane_of, source_depth = fifth & 3, (fifth >> 2) & 3
    core_of, target_depth = (fifth >> 4) & 1, fifth >> 5
    found = (
        (core_of * GROUP + plane_of) * block
        + (target_depth * GROUP + source_depth) * capacity
        + found_arrival
    )
    order = jnp.where(
        lax.broadcasted_iota(jnp.int32, (total, total), 1) == found, 1.0, 0.0
    ).astype(jnp.bfloat16)
    weight_copies[0].wait_recv()
    weight_copies[1].wait_recv()
    passed = [weight_copy(4, beside, 0, across), weight_copy(5, across, 1, beside)]
    for copy in passed:
        copy.start()

    for copy in place_copies:
        copy.wait()
    places = place_buf[0, 0:1, :]
    for j in range(1, GROUP):
        places = places + place_buf[j, 0:1, :]
    wanted = lax.broadcasted_iota(jnp.int32, (GROUP * block, GROUP * source_rows), 0)
    choice = jnp.where(wanted == places, 1.0, 0.0).astype(jnp.bfloat16)
    for copy in row_copies:
        copy.wait()
    owned = jnp.dot(
        row_buf[...].reshape(GROUP * source_rows, width), select,
        preferred_element_type=jnp.float32,
    ).astype(jnp.bfloat16)
    routed[...] = (
        jnp.dot(choice, owned, preferred_element_type=jnp.float32)
        .astype(jnp.bfloat16)
        .reshape(GROUP, block, GROUP * features)
    )
    mine = core * GROUP + plane
    routed_copies = [
        send(routed.at[ahead(plane, k)], arrived.at[mine], routed_send.at[k - 1],
             routed_recv.at[k - 1], along_plane(k, core))
        for k in range(1, GROUP)
    ]
    shared_copies = [
        send(routed.at[plane], arrived.at[mine], routed_send.at[last], routed_recv.at[last],
             (e, other))
    ]
    for copy in routed_copies + shared_copies:
        copy.start()
    arrived[mine] = routed[plane]
    context_step(1)
    for k in range(1, GROUP):
        routed_copies[k - 1].wait_recv()
        block_at = arrived.at[core * GROUP + ahead(plane, GROUP - k)]
        shared_copies.append(
            send(block_at, block_at, routed_send.at[last + k], routed_recv.at[last + k], (e, other))
        )
        shared_copies[-1].start()
    for copy in shared_copies:
        copy.wait()
    for copy in routed_copies:
        copy.wait_send()
    ordered = jnp.dot(
        order, arrived[...].reshape(total, GROUP * features), preferred_element_type=jnp.float32
    )
    grads[...] = ordered.astype(jnp.bfloat16).reshape(GROUP, slots, GROUP * features)
    context_step(2)

    for copy in weight_copies[2:] + passed:
        copy.wait()
    for copy in weight_copies[:2]:
        copy.wait_send()
    upper = depth // (GROUP // 2)

    def own_step(k, carry):
        at = upper * k + (1 - upper) * (last - k)
        context_own[at] = jnp.dot(
            grads[at], weights[...].reshape(GROUP * features, -1),
            preferred_element_type=jnp.float32,
        )
        return carry


    part_rows = slots // 2

    def sum_up(s, h):
        return send(up_out.at[s, h], up_in.at[s, h], gu_send.at[2 * s + h], gu_recv.at[2 * s + h],
                    ((depth + 1) * GROUP + plane, core))

    def sum_down(s, h):
        return send(down_out.at[s, h], down_in.at[s, h], gd_send.at[2 * s + h],
                    gd_recv.at[2 * s + h], ((depth - 1) * GROUP + plane, core))

    def up_wait(s, h):
        ref = up_in.at[s, h]
        send(ref, ref, gu_send.at[2 * s + h], gu_recv.at[2 * s + h], (e, other)).wait_recv()

    def down_wait(s, h):
        ref = down_in.at[s, h]
        send(ref, ref, gd_send.at[2 * s + h], gd_recv.at[2 * s + h], (e, other)).wait_recv()

    def sum_step(s, h):
        piece = slice(h * part_rows, (h + 1) * part_rows)

        @pl.when((depth < last) & (depth <= s))
        def _():
            at = last + depth - s
            if s == 0:
                up_out[s, h] = context_own[at, piece].astype(jnp.bfloat16)
            else:

                @pl.when(depth == 0)
                def _():
                    up_out[s, h] = context_own[at, piece].astype(jnp.bfloat16)

                @pl.when(depth > 0)
                def _():
                    up_wait(s - 1, h)
                    up_out[s, h] = (
                        context_own[at, piece] + up_in[s - 1, h].astype(jnp.float32)
                    ).astype(jnp.bfloat16)

            sum_up(s, h).start()

        @pl.when((depth > 0) & (last - depth <= s))
        def _():
            at = depth - last + s
            if s == 0:
                down_out[s, h] = context_own[at, piece].astype(jnp.bfloat16)
            else:

                @pl.when(depth == last)
                def _():
                    down_out[s, h] = context_own[at, piece].astype(jnp.bfloat16)

                @pl.when(depth < last)
                def _():
                    down_wait(s - 1, h)
                    down_out[s, h] = (
                        context_own[at, piece] + down_in[s - 1, h].astype(jnp.float32)
                    ).astype(jnp.bfloat16)

            sum_down(s, h).start()

    own_step(0, 0)
    sum_step(0, 0)
    sum_step(0, 1)
    lax.fori_loop(1, GROUP, own_step, 0)
    grads_t[...] = ordered.T.astype(jnp.bfloat16).reshape(GROUP, features, total)

    context_wait(2)

    def weight_step(at):
        weight_full[at] = jnp.dot(
            grads_t[at], contexts[...].reshape(total, -1), preferred_element_type=jnp.float32
        )

    def columns_of(at, h):
        return weight_full[at, :, h * half : (h + 1) * half]

    def gw_copy(index, to):
        return send(weight_out.at[index], weight_in.at[index], gw_send.at[index],
                    gw_recv.at[index], (depth * GROUP + to, core))

    gw_copies = [gw_copy(i, to) for i, to in enumerate((beside, across) * 2)]
    gw_copies += [gw_copy(4, across), gw_copy(5, beside)]

    def gw_start(index, value):
        weight_out[index] = value.astype(jnp.bfloat16)
        gw_copies[index].start()

    weight_step(corner)
    gw_start(0, columns_of(corner, 0))
    gw_start(1, columns_of(corner, 1))
    weight_step(beside)
    gw_start(2, columns_of(beside, 0))
    weight_step(across)
    gw_start(3, columns_of(across, 1))
    weight_step(plane)
    sum_step(1, 0)
    sum_step(1, 1)
    gw_copies[0].wait_recv()
    gw_start(4, columns_of(across, 0) + weight_in[0].astype(jnp.float32))
    gw_copies[1].wait_recv()
    gw_start(5, columns_of(beside, 1) + weight_in[1].astype(jnp.float32))
    sum_step(2, 0)
    sum_step(2, 1)
    for index in (2, 3, 4, 5):
        gw_copies[index].wait_recv()
    for copy in gw_copies:
        copy.wait_send()
    summed = jnp.concatenate(
        [
            columns_of(plane, h)
            + weight_in[2 + h].astype(jnp.float32)
            + weight_in[4 + h].astype(jnp.float32)
            for h in range(2)
        ],
        axis=1,
    )
    product = summed * weights[plane].astype(jnp.float32)
    lanes = product[:, :BLOCK]
    for j in range(1, product.shape[1] // BLOCK):
        lanes = lanes + product[:, j * BLOCK : (j + 1) * BLOCK]
    own = jnp.sum(lanes.T, axis=0, keepdims=True) * rescale
    pad = scale_plane.shape[2] - features
    own = jnp.broadcast_to(jnp.pad(own, ((0, 0), (0, pad))), scale_plane.shape[1:])

    scale_plane[mine] = own
    plane_copies = []
    for k in range(GROUP):
        for which, owner in enumerate((other, core)):
            if k > 0 or which == 0:
                index = 2 * k + which - (1 if k > 0 else 0)
                plane_copies.append(
                    send(scale_plane.at[mine], scale_plane.at[mine], plane_send.at[index],
                         plane_recv.at[index], along_plane(k, owner))
                )
    for copy in plane_copies:
        copy.start()
    grad_weight_ref[...] = summed[:share, :] * rescale
    for copy in plane_copies:
        copy.wait()
    for j in range(GROUP):
        scale_group[j] = scale_plane[j] + scale_plane[GROUP + j]
    all_copies = [
        send(scale_group, scale_all.at[depth], all_send.at[k - 1], all_recv.at[k - 1],
             along_depth(k))
        for k in range(1, GROUP)
    ]
    for copy in all_copies:
        copy.start()
    scale_all[depth] = scale_group[...]

    for h in range(2):
        piece = slice(h * part_rows, (h + 1) * part_rows)

        @pl.when(depth > 0)
        def _():
            up_wait(last - 1, h)
            context_own[depth, piece] += up_in[last - 1, h].astype(jnp.float32)

        @pl.when(depth < last)
        def _():
            down_wait(last - 1, h)
            context_own[depth, piece] += down_in[last - 1, h].astype(jnp.float32)

        grad_context_ref[piece, :] = context_own[depth, piece].astype(jnp.bfloat16)

    for s in range(last):

        @pl.when((depth < last) & (depth - s >= 0))
        def _():
            context_up(s).wait_send()

        @pl.when((depth > 0) & (depth + s <= last))
        def _():
            context_down(s).wait_send()

        @pl.when((depth < last) & (depth <= s))
        def _():
            for h in range(2):
                sum_up(s, h).wait_send()

        @pl.when((depth > 0) & (last - depth <= s))
        def _():
            for h in range(2):
                sum_down(s, h).wait_send()

    for copy in all_copies:
        copy.wait()
    whole = jnp.concatenate(
        [scale_all[d, q, 0:1, :share] for d in range(GROUP) for q in range(GROUP)], axis=1
    )
    scale_ref[...] = (whole / layer[...].reshape(1, -1)).reshape(-1)


def two_level(grad_rows, row_target, stored_context, block_scale, w_out, layer_scale):
    encoders = lax.axis_size("edata")
    owners = lax.axis_size("llm")
    source_rows, features = grad_rows.shape
    slot_count, columns = stored_context.shape
    capacity = slot_count // (encoders * owners)
    share = features // encoders
    padded = up(share, 16)
    starts = [d * GROUP * share // BLOCK * BLOCK for d in range(GROUP)]
    width = max(up((d + 1) * GROUP * share, BLOCK) - starts[d] for d in range(GROUP))
    block = GROUP * GROUP * capacity
    rescale = 1.0 / math.sqrt(source_rows * encoders * owners)

    total = GROUP * slot_count
    bf16, f32 = jnp.bfloat16, jnp.float32
    small = up(padded, 128)
    sems = [6, 3, 3, 3, 3, 6, 6, 7, 7, 3, 3, 3, 3, 6, 6, 6, 6, 6, 6, 7, 7, 3, 3]
    vmem = pl.BlockSpec(memory_space=pltpu.VMEM)
    far = pl.BlockSpec(memory_space=pltpu.HBM)
    return pl.pallas_call(
        functools.partial(kernel, capacity, rescale),
        out_shape=(
            pltpu.VMEM((slot_count, columns), bf16),
            pltpu.VMEM((share, columns), f32),
            pltpu.VMEM((features,), f32),
        ),
        in_specs=[far] * 6,
        out_specs=[vmem] * 3,
        scratch_shapes=[
            pltpu.VMEM((source_rows, features), bf16),
            pltpu.VMEM((source_rows, features), bf16),
            pltpu.VMEM((slot_count, columns), bf16),
            pltpu.VMEM((1, source_rows), jnp.int32),
            pltpu.VMEM((columns // BLOCK, slot_count), f32),
            pltpu.VMEM((share, columns), bf16),
            pltpu.VMEM((features,), f32),
            pltpu.VMEM((GROUP, source_rows, width), bf16),
            pltpu.VMEM((GROUP, 8, GROUP * source_rows), jnp.int32),
            pltpu.VMEM((GROUP, block, GROUP * padded), bf16),
            pltpu.VMEM((owners * GROUP, block, GROUP * padded), bf16),
            pltpu.VMEM((GROUP, slot_count, GROUP * padded), bf16),
            pltpu.VMEM((GROUP, padded, total), bf16),
            pltpu.VMEM((GROUP, slot_count, columns), bf16),
            pltpu.VMEM((GROUP, padded, columns), bf16),
            pltpu.VMEM((GROUP, slot_count, columns), f32),
            pltpu.VMEM((GROUP - 1, 2, slot_count // 2, columns), bf16),
            pltpu.VMEM((GROUP - 1, 2, slot_count // 2, columns), bf16),
            pltpu.VMEM((GROUP - 1, 2, slot_count // 2, columns), bf16),
            pltpu.VMEM((GROUP - 1, 2, slot_count // 2, columns), bf16),
            pltpu.VMEM((GROUP, padded, columns), f32),
            pltpu.VMEM((6, padded, columns // 2), bf16),
            pltpu.VMEM((6, padded, columns // 2), bf16),
            pltpu.VMEM((owners * GROUP, 8, small), f32),
            pltpu.VMEM((GROUP, 8, small), f32),
            pltpu.VMEM((GROUP, GROUP, 8, small), f32),
        ]
        + [pltpu.SemaphoreType.DMA((n,)) for n in sems],
        compiler_params=pltpu.CompilerParams(
            collective_id=0, has_side_effects=True, vmem_limit_bytes=48 * 2**20
        ),
    )(
        *[
            pltpu.with_memory_space_constraint(array, pltpu.HBM)
            for array in (
                grad_rows, row_target.T, stored_context, block_scale.T, w_out.T, layer_scale
            )
        ]
    )


def on_device(grad_rows, row_target, stored_context, block_scale, w_out, layer_scale):
    encoders = lax.axis_size("edata")
    owners = lax.axis_size("llm")
    source_rows = grad_rows.shape[0]
    features = grad_rows.shape[1]
    slot_count = stored_context.shape[0]
    capacity = slot_count // (encoders * owners)
    weights = lax.all_gather(w_out, "edata", axis=1, tiled=True)
    targets = row_target[:, 0]
    chosen = (targets[:, None] == jnp.arange(encoders, dtype=jnp.int32)[None, :]).astype(jnp.int32)
    arrival = jnp.sum(chosen * (jnp.cumsum(chosen, axis=0) - 1), axis=1)
    position = targets * capacity + arrival
    outgoing = jnp.zeros((encoders * capacity, features), jnp.bfloat16).at[position].set(grad_rows)
    arrived = lax.all_to_all(outgoing, "edata", split_axis=0, concat_axis=0, tiled=True)
    grad_slots = lax.all_gather(arrived, "llm", axis=0, tiled=True)
    stored = stored_context.astype(jnp.float32).reshape(slot_count, -1, BLOCK)
    context = (stored * block_scale[:, :, None]).reshape(slot_count, -1).astype(jnp.bfloat16)
    scaled = (grad_slots.astype(jnp.float32) * layer_scale[None, :]).astype(jnp.bfloat16)
    recomputed = jnp.dot(context, weights, preferred_element_type=jnp.float32)
    grad_context = lax.dot_general(
        scaled, weights, (((1,), (1,)), ((), ())), preferred_element_type=jnp.float32
    ).astype(jnp.bfloat16)
    partial_scale = jnp.sum(grad_slots.astype(jnp.float32) * recomputed, axis=0)
    rescale = 1.0 / math.sqrt(source_rows * encoders * owners)
    grad_weight = (
        lax.psum_scatter(
            lax.dot_general(
                scaled, context, (((0,), (0,)), ((), ())), preferred_element_type=jnp.float32
            ),
            "edata",
            scatter_dimension=0,
            tiled=True,
        )
        * rescale
    )
    grad_scale = lax.psum(partial_scale, ("edata", "llm")) * rescale
    return (grad_context, grad_weight, grad_scale)


def solution(mesh):
    in_specs = (
        P(("edata", "llm"), None),
        P(("edata", "llm"), None),
        P("edata", "llm"),
        P("edata", "llm"),
        P("llm", "edata"),
        P(),
    )
    out_specs = (P("edata", "llm"), P("edata", "llm"), P())
    two_levels = mesh.shape["edata"] == GROUP * GROUP and mesh.shape["llm"] == 2
    return jax.shard_map(
        two_level if two_levels else on_device, mesh=mesh, in_specs=in_specs, out_specs=out_specs, check_vma=False
    )
```

```python
import functools
import math

import jax
import jax.numpy as jnp
from jax import lax
from jax.experimental import pallas as pl
from jax.experimental.pallas import tpu as pltpu
from jax.sharding import PartitionSpec as P

BLOCK = 128
GROUP = 4
MESH = pl.DeviceIdType.MESH


def up(value, unit):
    return -(-value // unit) * unit


def kernel(
    capacity, rescale, gradient_ref, target_ref, stored_ref, block_ref, weight_in_ref, layer_in_ref,
    grad_context_ref, grad_weight_ref, scale_ref,
    gradient, scaled, stored, targets, blocks, weight_own, layer, row_buf, place_buf, routed, arrived, grads, grads_t, contexts,
    weights, context_own, up_out, up_in, down_out, down_in, weight_full, weight_out, weight_in,
    scale_plane, scale_group, scale_all,
    load_sem, row_send, row_recv, place_send, place_recv, weight_send, weight_recv,
    routed_send, routed_recv, cu_send, cu_recv, cd_send, cd_recv, gu_send, gu_recv,
    gd_send, gd_recv, gw_send, gw_recv, plane_send, plane_recv, all_send, all_recv,
):
    e, core = lax.axis_index("edata"), lax.axis_index("llm")
    depth, plane = e // GROUP, e % GROUP
    other = 1 - core
    last = GROUP - 1
    share = weight_own.shape[0]
    features = weights.shape[1]
    slots = stored.shape[0]
    block = routed.shape[1]
    source_rows, width = row_buf.shape[1:]

    def ahead(own, k):
        return (own + k) % GROUP

    def along_depth(k):
        return (ahead(depth, k) * GROUP + plane, core)

    def along_plane(k, owner):
        return (depth * GROUP + ahead(plane, k), owner)

    def send(src, dst, send_sem, recv_sem, device):
        return pltpu.make_async_remote_copy(
            src_ref=src, dst_ref=dst, send_sem=send_sem, recv_sem=recv_sem,
            device_id=device, device_id_type=MESH,
        )

    loads = [
        pltpu.make_async_copy(gradient_ref, gradient, load_sem.at[0]),
        pltpu.make_async_copy(layer_in_ref, layer, load_sem.at[1]),
        pltpu.make_async_copy(target_ref, targets, load_sem.at[2]),
        pltpu.make_async_copy(weight_in_ref, weight_own, load_sem.at[3]),
        pltpu.make_async_copy(stored_ref, stored, load_sem.at[4]),
        pltpu.make_async_copy(block_ref, blocks, load_sem.at[5]),
    ]
    for copy in loads:
        copy.start()
    barrier = pltpu.get_barrier_semaphore()
    for k in range(1, GROUP):
        pl.semaphore_signal(barrier, inc=1, device_id=along_depth(k), device_id_type=MESH)
        for owner in (core, other):
            pl.semaphore_signal(
                barrier, inc=1, device_id=along_plane(k, owner), device_id_type=MESH
            )
    pl.semaphore_signal(barrier, inc=1, device_id=(e, other), device_id_type=MESH)

    loads[2].wait()
    target = jnp.broadcast_to(targets[...], (source_rows, source_rows))
    first = lax.broadcasted_iota(jnp.int32, (source_rows, source_rows), 0)
    second = lax.broadcasted_iota(jnp.int32, (source_rows, source_rows), 1)
    column = target.astype(jnp.float32).T.astype(jnp.int32)
    before = jnp.where((target == column) & (first < second), 1.0, 0.0)
    arrival = jnp.sum(before, axis=0, keepdims=True).astype(jnp.int32)
    target = targets[...]
    place = (target & 3) * block + ((target >> 2) * GROUP + depth) * capacity + arrival
    spread = jnp.concatenate([place] * GROUP, axis=1)
    lane = lax.broadcasted_iota(jnp.int32, spread.shape, 1)
    begin = depth * source_rows
    inside = (lane >= begin) & (lane < begin + source_rows)
    place_buf[depth] = jnp.broadcast_to(jnp.where(inside, spread, 0), place_buf.shape[1:])
    loads[3].wait()
    weights[plane, :share, :] = weight_own[...]
    weights[plane, share:, :] = jnp.zeros((features - share, weights.shape[2]), weights.dtype)
    loads[0].wait()
    loads[1].wait()
    scaled[...] = (gradient[...].astype(jnp.float32) * layer[...].reshape(1, -1)).astype(jnp.bfloat16)
    pl.semaphore_wait(barrier, 3 * last + 1)

    def window(at):
        return pl.multiple_of((at * (GROUP * share)) // BLOCK * BLOCK, BLOCK)

    row_copies = []
    place_copies = []
    for k in range(1, GROUP):
        row_copies.append(
            send(scaled.at[:, pl.ds(window(ahead(depth, k)), width)], row_buf.at[depth],
                 row_send.at[k - 1], row_recv.at[k - 1], along_depth(k))
        )
        place_copies.append(
            send(place_buf.at[depth], place_buf.at[depth],
                 place_send.at[k - 1], place_recv.at[k - 1], along_depth(k))
        )
    for copy in place_copies + row_copies:
        copy.start()
    half = weights.shape[2] // 2
    beside = plane // 2 * 2 + (1 - plane % 2)
    corner = last - plane
    across = (1 - plane // 2) * 2 + plane % 2

    def weight_copy(index, owner, part, to):
        ref = weights.at[owner, :, pl.ds(part * half, half)]
        return send(ref, ref, weight_send.at[index], weight_recv.at[index],
                    (depth * GROUP + to, core))

    weight_copies = [
        weight_copy(0, plane, 0, beside),
        weight_copy(1, plane, 1, across),
        weight_copy(2, plane, 1, beside),
        weight_copy(3, plane, 0, across),
    ]
    for copy in weight_copies:
        copy.start()
    row_buf[depth] = scaled[:, pl.ds(window(depth), width)]

    loads[4].wait()
    loads[5].wait()
    factors = blocks[...].T
    for j in range(factors.shape[1]):
        part = slice(j * BLOCK, (j + 1) * BLOCK)
        contexts[depth, :, part] = (
            stored[:, part].astype(jnp.float32) * factors[:, j : j + 1]
        ).astype(jnp.bfloat16)

    def context_up(s):
        return send(contexts.at[depth - s], contexts.at[depth - s], cu_send.at[s],
                    cu_recv.at[s], ((depth + 1) * GROUP + plane, core))

    def context_down(s):
        return send(contexts.at[depth + s], contexts.at[depth + s], cd_send.at[s],
                    cd_recv.at[s], ((depth - 1) * GROUP + plane, core))

    def context_wait(s):
        @pl.when(depth - 1 - s >= 0)
        def _():
            below = contexts.at[depth - 1 - s]
            send(below, below, cu_send.at[s], cu_recv.at[s], (e, other)).wait_recv()

        @pl.when(depth + 1 + s <= last)
        def _():
            above = contexts.at[depth + 1 + s]
            send(above, above, cd_send.at[s], cd_recv.at[s], (e, other)).wait_recv()

    def context_step(s):
        if s > 0:
            context_wait(s - 1)

        @pl.when((depth < last) & (depth - s >= 0))
        def _():
            context_up(s).start()

        @pl.when((depth > 0) & (depth + s <= last))
        def _():
            context_down(s).start()

    context_step(0)

    lane = lax.broadcasted_iota(jnp.int32, (1, GROUP * features), 1)
    part = jnp.zeros_like(lane)
    for k in range(1, GROUP):
        part = part + jnp.where(lane >= k * features, 1, 0)
    within = lane - part * features
    source = depth * (GROUP * share) - window(depth) + part * share + within
    source = jnp.where(within < share, source, -1)
    select = jnp.where(
        lax.broadcasted_iota(jnp.int32, (width, GROUP * features), 0) == source, 1.0, 0.0
    ).astype(jnp.bfloat16)

    total = GROUP * slots
    slot = lax.broadcasted_iota(jnp.int32, (total, 1), 0)
    fifth = (slot * (2**18 // capacity + 1)) >> 18
    found_arrival = slot - fifth * capacity
    plane_of, source_depth = fifth & 3, (fifth >> 2) & 3
    core_of, target_depth = (fifth >> 4) & 1, fifth >> 5
    found = (
        (core_of * GROUP + plane_of) * block
        + (target_depth * GROUP + source_depth) * capacity
        + found_arrival
    )
    order = jnp.where(
        lax.broadcasted_iota(jnp.int32, (total, total), 1) == found, 1.0, 0.0
    ).astype(jnp.bfloat16)
    weight_copies[0].wait_recv()
    weight_copies[1].wait_recv()
    passed = [weight_copy(4, beside, 0, across), weight_copy(5, across, 1, beside)]
    for copy in passed:
        copy.start()

    for copy in place_copies:
        copy.wait()
    places = place_buf[0, 0:1, :]
    for j in range(1, GROUP):
        places = places + place_buf[j, 0:1, :]
    wanted = lax.broadcasted_iota(jnp.int32, (GROUP * block, GROUP * source_rows), 0)
    choice = jnp.where(wanted == places, 1.0, 0.0).astype(jnp.bfloat16)
    for copy in row_copies:
        copy.wait()
    owned = jnp.dot(
        row_buf[...].reshape(GROUP * source_rows, width), select,
        preferred_element_type=jnp.float32,
    ).astype(jnp.bfloat16)
    routed[...] = (
        jnp.dot(choice, owned, preferred_element_type=jnp.float32)
        .astype(jnp.bfloat16)
        .reshape(GROUP, block, GROUP * features)
    )
    mine = core * GROUP + plane
    routed_copies = [
        send(routed.at[ahead(plane, k)], arrived.at[mine], routed_send.at[k - 1],
             routed_recv.at[k - 1], along_plane(k, core))
        for k in range(1, GROUP)
    ]
    shared_copies = [
        send(routed.at[plane], arrived.at[mine], routed_send.at[last], routed_recv.at[last],
             (e, other))
    ]
    for copy in routed_copies + shared_copies:
        copy.start()
    arrived[mine] = routed[plane]
    context_step(1)
    for k in range(1, GROUP):
        routed_copies[k - 1].wait_recv()
        block_at = arrived.at[core * GROUP + ahead(plane, GROUP - k)]
        shared_copies.append(
            send(block_at, block_at, routed_send.at[last + k], routed_recv.at[last + k], (e, other))
        )
        shared_copies[-1].start()
    for copy in shared_copies:
        copy.wait()
    for copy in routed_copies:
        copy.wait_send()
    ordered = jnp.dot(
        order, arrived[...].reshape(total, GROUP * features), preferred_element_type=jnp.float32
    )
    grads[...] = ordered.astype(jnp.bfloat16).reshape(GROUP, slots, GROUP * features)
    context_step(2)

    for copy in weight_copies[2:] + passed:
        copy.wait()
    for copy in weight_copies[:2]:
        copy.wait_send()
    upper = depth // (GROUP // 2)

    def own_step(k, carry):
        at = upper * k + (1 - upper) * (last - k)
        context_own[at] = jnp.dot(
            grads[at], weights[...].reshape(GROUP * features, -1),
            preferred_element_type=jnp.float32,
        )
        return carry


    part_rows = slots // 2

    def sum_up(s, h):
        return send(up_out.at[s, h], up_in.at[s, h], gu_send.at[2 * s + h], gu_recv.at[2 * s + h],
                    ((depth + 1) * GROUP + plane, core))

    def sum_down(s, h):
        return send(down_out.at[s, h], down_in.at[s, h], gd_send.at[2 * s + h],
                    gd_recv.at[2 * s + h], ((depth - 1) * GROUP + plane, core))

    def up_wait(s, h):
        ref = up_in.at[s, h]
        send(ref, ref, gu_send.at[2 * s + h], gu_recv.at[2 * s + h], (e, other)).wait_recv()

    def down_wait(s, h):
        ref = down_in.at[s, h]
        send(ref, ref, gd_send.at[2 * s + h], gd_recv.at[2 * s + h], (e, other)).wait_recv()

    def sum_step(s, h):
        piece = slice(h * part_rows, (h + 1) * part_rows)

        @pl.when((depth < last) & (depth <= s))
        def _():
            at = last + depth - s
            if s == 0:
                up_out[s, h] = context_own[at, piece].astype(jnp.bfloat16)
            else:

                @pl.when(depth == 0)
                def _():
                    up_out[s, h] = context_own[at, piece].astype(jnp.bfloat16)

                @pl.when(depth > 0)
                def _():
                    up_wait(s - 1, h)
                    up_out[s, h] = (
                        context_own[at, piece] + up_in[s - 1, h].astype(jnp.float32)
                    ).astype(jnp.bfloat16)

            sum_up(s, h).start()

        @pl.when((depth > 0) & (last - depth <= s))
        def _():
            at = depth - last + s
            if s == 0:
                down_out[s, h] = context_own[at, piece].astype(jnp.bfloat16)
            else:

                @pl.when(depth == last)
                def _():
                    down_out[s, h] = context_own[at, piece].astype(jnp.bfloat16)

                @pl.when(depth < last)
                def _():
                    down_wait(s - 1, h)
                    down_out[s, h] = (
                        context_own[at, piece] + down_in[s - 1, h].astype(jnp.float32)
                    ).astype(jnp.bfloat16)

            sum_down(s, h).start()

    own_step(0, 0)
    sum_step(0, 0)
    sum_step(0, 1)
    grads_t[...] = ordered.T.astype(jnp.bfloat16).reshape(GROUP, features, total)

    context_wait(2)

    def weight_step(at):
        weight_full[at] = jnp.dot(
            grads_t[at], contexts[...].reshape(total, -1), preferred_element_type=jnp.float32
        )

    def columns_of(at, h):
        return weight_full[at, :, h * half : (h + 1) * half]

    def gw_copy(index, to):
        return send(weight_out.at[index], weight_in.at[index], gw_send.at[index],
                    gw_recv.at[index], (depth * GROUP + to, core))

    gw_copies = [gw_copy(i, to) for i, to in enumerate((beside, across) * 2)]
    gw_copies += [gw_copy(4, across), gw_copy(5, beside)]

    def gw_start(index, value):
        weight_out[index] = value.astype(jnp.bfloat16)
        gw_copies[index].start()

    weight_step(corner)
    gw_start(0, columns_of(corner, 0))
    gw_start(1, columns_of(corner, 1))
    weight_step(beside)
    gw_start(2, columns_of(beside, 0))
    weight_step(across)
    gw_start(3, columns_of(across, 1))
    lax.fori_loop(1, GROUP, own_step, 0)
    sum_step(1, 0)
    sum_step(1, 1)
    weight_step(plane)
    gw_copies[0].wait_recv()
    gw_start(4, columns_of(across, 0) + weight_in[0].astype(jnp.float32))
    gw_copies[1].wait_recv()
    gw_start(5, columns_of(beside, 1) + weight_in[1].astype(jnp.float32))
    sum_step(2, 0)
    sum_step(2, 1)
    for index in (2, 3, 4, 5):
        gw_copies[index].wait_recv()
    for copy in gw_copies:
        copy.wait_send()
    summed = jnp.concatenate(
        [
            columns_of(plane, h)
            + weight_in[2 + h].astype(jnp.float32)
            + weight_in[4 + h].astype(jnp.float32)
            for h in range(2)
        ],
        axis=1,
    )
    product = summed * weights[plane].astype(jnp.float32)
    lanes = product[:, :BLOCK]
    for j in range(1, product.shape[1] // BLOCK):
        lanes = lanes + product[:, j * BLOCK : (j + 1) * BLOCK]
    own = jnp.sum(lanes.T, axis=0, keepdims=True) * rescale
    pad = scale_plane.shape[2] - features
    own = jnp.broadcast_to(jnp.pad(own, ((0, 0), (0, pad))), scale_plane.shape[1:])

    scale_plane[mine] = own
    plane_copies = []
    for k in range(GROUP):
        for which, owner in enumerate((other, core)):
            if k > 0 or which == 0:
                index = 2 * k + which - (1 if k > 0 else 0)
                plane_copies.append(
                    send(scale_plane.at[mine], scale_plane.at[mine], plane_send.at[index],
                         plane_recv.at[index], along_plane(k, owner))
                )
    for copy in plane_copies:
        copy.start()
    grad_weight_ref[...] = summed[:share, :] * rescale
    for copy in plane_copies:
        copy.wait()
    for j in range(GROUP):
        scale_group[j] = scale_plane[j] + scale_plane[GROUP + j]
    all_copies = [
        send(scale_group, scale_all.at[depth], all_send.at[k - 1], all_recv.at[k - 1],
             along_depth(k))
        for k in range(1, GROUP)
    ]
    for copy in all_copies:
        copy.start()
    scale_all[depth] = scale_group[...]

    for h in range(2):
        piece = slice(h * part_rows, (h + 1) * part_rows)

        @pl.when(depth > 0)
        def _():
            up_wait(last - 1, h)
            context_own[depth, piece] += up_in[last - 1, h].astype(jnp.float32)

        @pl.when(depth < last)
        def _():
            down_wait(last - 1, h)
            context_own[depth, piece] += down_in[last - 1, h].astype(jnp.float32)

        grad_context_ref[piece, :] = context_own[depth, piece].astype(jnp.bfloat16)

    for s in range(last):

        @pl.when((depth < last) & (depth - s >= 0))
        def _():
            context_up(s).wait_send()

        @pl.when((depth > 0) & (depth + s <= last))
        def _():
            context_down(s).wait_send()

        @pl.when((depth < last) & (depth <= s))
        def _():
            for h in range(2):
                sum_up(s, h).wait_send()

        @pl.when((depth > 0) & (last - depth <= s))
        def _():
            for h in range(2):
                sum_down(s, h).wait_send()

    for copy in all_copies:
        copy.wait()
    whole = jnp.concatenate(
        [scale_all[d, q, 0:1, :share] for d in range(GROUP) for q in range(GROUP)], axis=1
    )
    scale_ref[...] = (whole / layer[...].reshape(1, -1)).reshape(-1)


def two_level(grad_rows, row_target, stored_context, block_scale, w_out, layer_scale):
    encoders = lax.axis_size("edata")
    owners = lax.axis_size("llm")
    source_rows, features = grad_rows.shape
    slot_count, columns = stored_context.shape
    capacity = slot_count // (encoders * owners)
    share = features // encoders
    padded = up(share, 16)
    starts = [d * GROUP * share // BLOCK * BLOCK for d in range(GROUP)]
    width = max(up((d + 1) * GROUP * share, BLOCK) - starts[d] for d in range(GROUP))
    block = GROUP * GROUP * capacity
    rescale = 1.0 / math.sqrt(source_rows * encoders * owners)

    total = GROUP * slot_count
    bf16, f32 = jnp.bfloat16, jnp.float32
    small = up(padded, 128)
    sems = [6, 3, 3, 3, 3, 6, 6, 7, 7, 3, 3, 3, 3, 6, 6, 6, 6, 6, 6, 7, 7, 3, 3]
    vmem = pl.BlockSpec(memory_space=pltpu.VMEM)
    far = pl.BlockSpec(memory_space=pltpu.HBM)
    return pl.pallas_call(
        functools.partial(kernel, capacity, rescale),
        out_shape=(
            pltpu.VMEM((slot_count, columns), bf16),
            pltpu.VMEM((share, columns), f32),
            pltpu.VMEM((features,), f32),
        ),
        in_specs=[far] * 6,
        out_specs=[vmem] * 3,
        scratch_shapes=[
            pltpu.VMEM((source_rows, features), bf16),
            pltpu.VMEM((source_rows, features), bf16),
            pltpu.VMEM((slot_count, columns), bf16),
            pltpu.VMEM((1, source_rows), jnp.int32),
            pltpu.VMEM((columns // BLOCK, slot_count), f32),
            pltpu.VMEM((share, columns), bf16),
            pltpu.VMEM((features,), f32),
            pltpu.VMEM((GROUP, source_rows, width), bf16),
            pltpu.VMEM((GROUP, 8, GROUP * source_rows), jnp.int32),
            pltpu.VMEM((GROUP, block, GROUP * padded), bf16),
            pltpu.VMEM((owners * GROUP, block, GROUP * padded), bf16),
            pltpu.VMEM((GROUP, slot_count, GROUP * padded), bf16),
            pltpu.VMEM((GROUP, padded, total), bf16),
            pltpu.VMEM((GROUP, slot_count, columns), bf16),
            pltpu.VMEM((GROUP, padded, columns), bf16),
            pltpu.VMEM((GROUP, slot_count, columns), f32),
            pltpu.VMEM((GROUP - 1, 2, slot_count // 2, columns), bf16),
            pltpu.VMEM((GROUP - 1, 2, slot_count // 2, columns), bf16),
            pltpu.VMEM((GROUP - 1, 2, slot_count // 2, columns), bf16),
            pltpu.VMEM((GROUP - 1, 2, slot_count // 2, columns), bf16),
            pltpu.VMEM((GROUP, padded, columns), f32),
            pltpu.VMEM((6, padded, columns // 2), bf16),
            pltpu.VMEM((6, padded, columns // 2), bf16),
            pltpu.VMEM((owners * GROUP, 8, small), f32),
            pltpu.VMEM((GROUP, 8, small), f32),
            pltpu.VMEM((GROUP, GROUP, 8, small), f32),
        ]
        + [pltpu.SemaphoreType.DMA((n,)) for n in sems],
        compiler_params=pltpu.CompilerParams(
            collective_id=0, has_side_effects=True, vmem_limit_bytes=48 * 2**20
        ),
    )(
        *[
            pltpu.with_memory_space_constraint(array, pltpu.HBM)
            for array in (
                grad_rows, row_target.T, stored_context, block_scale.T, w_out.T, layer_scale
            )
        ]
    )


def on_device(grad_rows, row_target, stored_context, block_scale, w_out, layer_scale):
    encoders = lax.axis_size("edata")
    owners = lax.axis_size("llm")
    source_rows = grad_rows.shape[0]
    features = grad_rows.shape[1]
    slot_count = stored_context.shape[0]
    capacity = slot_count // (encoders * owners)
    weights = lax.all_gather(w_out, "edata", axis=1, tiled=True)
    targets = row_target[:, 0]
    chosen = (targets[:, None] == jnp.arange(encoders, dtype=jnp.int32)[None, :]).astype(jnp.int32)
    arrival = jnp.sum(chosen * (jnp.cumsum(chosen, axis=0) - 1), axis=1)
    position = targets * capacity + arrival
    outgoing = jnp.zeros((encoders * capacity, features), jnp.bfloat16).at[position].set(grad_rows)
    arrived = lax.all_to_all(outgoing, "edata", split_axis=0, concat_axis=0, tiled=True)
    grad_slots = lax.all_gather(arrived, "llm", axis=0, tiled=True)
    stored = stored_context.astype(jnp.float32).reshape(slot_count, -1, BLOCK)
    context = (stored * block_scale[:, :, None]).reshape(slot_count, -1).astype(jnp.bfloat16)
    scaled = (grad_slots.astype(jnp.float32) * layer_scale[None, :]).astype(jnp.bfloat16)
    recomputed = jnp.dot(context, weights, preferred_element_type=jnp.float32)
    grad_context = lax.dot_general(
        scaled, weights, (((1,), (1,)), ((), ())), preferred_element_type=jnp.float32
    ).astype(jnp.bfloat16)
    partial_scale = jnp.sum(grad_slots.astype(jnp.float32) * recomputed, axis=0)
    rescale = 1.0 / math.sqrt(source_rows * encoders * owners)
    grad_weight = (
        lax.psum_scatter(
            lax.dot_general(
                scaled, context, (((0,), (0,)), ((), ())), preferred_element_type=jnp.float32
            ),
            "edata",
            scatter_dimension=0,
            tiled=True,
        )
        * rescale
    )
    grad_scale = lax.psum(partial_scale, ("edata", "llm")) * rescale
    return (grad_context, grad_weight, grad_scale)


def solution(mesh):
    in_specs = (
        P(("edata", "llm"), None),
        P(("edata", "llm"), None),
        P("edata", "llm"),
        P("edata", "llm"),
        P("llm", "edata"),
        P(),
    )
    out_specs = (P("edata", "llm"), P("edata", "llm"), P())
    two_levels = mesh.shape["edata"] == GROUP * GROUP and mesh.shape["llm"] == 2
    return jax.shard_map(
        two_level if two_levels else on_device, mesh=mesh, in_specs=in_specs, out_specs=out_specs, check_vma=False
    )
```
